128 devices in a mesh: expert: 4 (over y), shard: 32 (over z, x, core).
Axes of the slice: x: 4, y: 4, z: 4, core: 2. Of those that a mesh axis runs over, the one named last changes fastest.
Arguments:
- gradient: float32 [4, 32, 512, 512], P('expert', None, 'shard')
- left_stat: float32 [4, 96, 512, 512], P('expert', 'shard'), as said below
- right_stat: float32 [4, 96, 512, 512], P('expert', 'shard'), as said below
- assign: int32 [4, 96], P('expert'), may hold values from -1 to 31, as said below
Outputs:
- update: float32 [4, 32, 512, 512], P('expert', None, 'shard')
- new_left: float32 [4, 96, 512, 512], P('expert', 'shard')
- new_right: float32 [4, 96, 512, 512], P('expert', 'shard')
The draws below stay inside these ranges and needn't reach their ends.
Inputs may be any that keep to these rules, and one draw needn't show every extreme that they name: `assign`: slots d * 3 to d * 3 + 2 are those of device d of shard; each holds a block id or -1, the ids first and the -1 after. Every block of an expert is in exactly one slot. In every expert some device holds 3 blocks. `left_stat`: symmetric positive definite. `right_stat`: symmetric positive definite.
All inputs are finite; a program needn't handle non-finite values.
Results may differ from the reference program's by a relative error of at most 0.00018.
Values sent between devices are 32-bit elements; how exact they have to be, the bound alone decides.
A program may use at most 128 MiB of HBM per device.

```python
import jax
import jax.numpy as jnp
from jax import lax

BLOCK = 512
NBLK = 32
MAXOWN = 3
SLOTS = 96
EXPERTS = 4


def symmetric_stat(key, low_value, high_value, peak_coef, reach_div, weight_low, weight_high):
    key_diag, key_off, key_weight = jax.random.split(key, 3)
    shape = (EXPERTS, SLOTS, BLOCK, BLOCK)
    diagonal = jnp.exp(jax.random.uniform(key_diag, (EXPERTS, SLOTS, BLOCK), jnp.float32, jnp.log(low_value), jnp.log(high_value)))
    raw_noise = jax.random.truncated_normal(key_off, -3.0, 3.0, shape, jnp.float32)
    mixed = (raw_noise + jnp.swapaxes(raw_noise, -1, -2)) * 0.7071
    root_diag = jnp.sqrt(diagonal)
    identity = jnp.eye(BLOCK, dtype=jnp.float32)
    matrix = 0.012 * mixed * root_diag[..., :, None] * root_diag[..., None, :]
    weights = jnp.exp(jax.random.uniform(key_weight, (EXPERTS, SLOTS, BLOCK), jnp.float32, jnp.log(weight_low), jnp.log(weight_high)))
    position = jnp.arange(BLOCK, dtype=jnp.float32)
    distance = jnp.abs(position[:, None] - position[None, :])
    kernel = jnp.exp(-distance * (reach_div / BLOCK))
    peak = peak_coef * jnp.sqrt(jnp.float32(BLOCK))
    coupled = peak * weights[..., :, None] * weights[..., None, :] * kernel
    return matrix * (1.0 - identity) + diagonal[..., :, None] * identity + coupled


def draw_left_stat(key, part):
    key = jax.random.fold_in(key, 5)
    return symmetric_stat(key, 100.0, 1000.0, 19.0, 6.0, 0.5, 2.0)


def draw_right_stat(key, part):
    key = jax.random.fold_in(key, 9)
    return symmetric_stat(key, 100.0, 1000.0, 19.0, 6.0, 0.5, 2.0)


def draw_gradient(key, part):
    key = jax.random.fold_in(key, 7)
    key_noise, key_rows, key_cols = jax.random.split(key, 3)
    shape = (EXPERTS, NBLK, BLOCK, BLOCK)
    noise = jax.random.normal(key_noise, shape, jnp.float32)
    spread = jnp.log(10.0)
    row_scale = jnp.exp(jax.random.uniform(key_rows, (EXPERTS, NBLK, BLOCK, 1), jnp.float32) * spread)
    col_scale = jnp.exp(jax.random.uniform(key_cols, (EXPERTS, NBLK, 1, BLOCK), jnp.float32) * spread)
    level = (jnp.arange(EXPERTS, dtype=jnp.float32)[:, None] * BLOCK + jnp.arange(BLOCK, dtype=jnp.float32)[None, :]) / (2.0 * EXPERTS * BLOCK)
    trend = jnp.exp(jnp.log(3.0) * level)[:, None, :, None]
    return noise * row_scale * col_scale * trend * 0.125


def owner_table(key):
    key_heavy, key_order, key_blocks = jax.random.split(key, 3)
    devices = SLOTS // MAXOWN
    heavy = jax.random.randint(key_heavy, (), 0, devices)
    device_of = jnp.arange(SLOTS, dtype=jnp.int32) // MAXOWN
    scores = jax.random.permutation(key_order, SLOTS).astype(jnp.int32)
    scores = scores + jnp.where(device_of == heavy, SLOTS, 0).astype(jnp.int32)
    chosen_index = lax.top_k(scores, NBLK)[1]
    chosen = jnp.zeros((SLOTS,), jnp.int32).at[chosen_index].set(1)
    position = (jnp.cumsum(chosen.reshape(devices, MAXOWN), axis=1) - 1).reshape(-1)
    rank_all = jnp.cumsum(chosen) - 1
    block_order = jax.random.permutation(key_blocks, NBLK).astype(jnp.int32)
    target = jnp.where(chosen == 1, device_of * MAXOWN + position, SLOTS)
    values = block_order[jnp.clip(rank_all, 0, NBLK - 1)]
    return jnp.full((SLOTS,), -1, jnp.int32).at[target].set(values, mode='drop')


def draw_assign(key, part):
    key = jax.random.fold_in(key, 3)
    tables = [owner_table(jax.random.fold_in(key, expert)) for expert in range(EXPERTS)]
    return jnp.stack(tables)


def setup_inputs(seed: int = 0) -> dict:
    key_of = jax.random.split(jax.random.key(seed), 5)
    gradient = draw_gradient(jax.random.fold_in(key_of[4], 71), 0)
    left_stat = draw_left_stat(jax.random.fold_in(key_of[4], 71), 0)
    right_stat = draw_right_stat(jax.random.fold_in(key_of[4], 71), 0)
    assign = draw_assign(jax.random.fold_in(key_of[4], 71), 0)
    return dict(gradient=gradient, left_stat=left_stat, right_stat=right_stat, assign=assign)


beta_decay = 0.95
clip_rms = 1.0

def product(left_mat, right_mat):
    return jnp.dot(left_mat, right_mat, precision=lax.Precision.HIGHEST, preferred_element_type=jnp.float32)

def inverse_root(matrix):
    identity = jnp.eye(matrix.shape[0], dtype=jnp.float32)
    norm_fourth = jnp.sqrt(jnp.sum(matrix * matrix) + 1e-06)
    root_scale = jnp.sqrt(jnp.sqrt(norm_fourth))
    scaled_start = matrix / norm_fourth
    first_step = (5.0 * identity - scaled_start) * 0.25
    square = product(first_step, first_step)
    fourth = product(square, square)
    moved_mat = product(fourth, scaled_start)
    second_step = (5.0 * identity - moved_mat) * 0.25
    return product(first_step / root_scale, second_step)

def precondition(scaled, left_new, right_new):
    precond = product(product(inverse_root(left_new), scaled), inverse_root(right_new))
    graft_ratio = jnp.sqrt(jnp.mean(scaled * scaled) + 1e-12) / jnp.sqrt(jnp.mean(precond * precond) + 1e-12)
    return precond * graft_ratio

def reference(gradient, left_stat, right_stat, assign):
    factor = jnp.minimum(1.0, clip_rms / jnp.sqrt(jnp.mean(gradient * gradient) + 1e-06))
    update_list, left_list, right_list = ([], [], [])
    for expert in range(EXPERTS):
        assign_row = assign[expert]
        block_ids = jnp.arange(NBLK, dtype=jnp.int32)
        slot_index = jnp.arange(SLOTS, dtype=jnp.int32)
        slot_of_block = lax.optimization_barrier(jnp.sum(jnp.where(assign_row[None, :] == block_ids[:, None], slot_index[None, :], 0), axis=1)).astype(jnp.int32)

        def one_block(block_items):
            grad_block, left_mat, right_mat = block_items
            scaled = factor * grad_block
            left_new = beta_decay * left_mat + product(scaled, scaled.T)
            right_new = beta_decay * right_mat + product(scaled.T, scaled)
            return (precondition(scaled, left_new, right_new), left_new, right_new)
        precond, left_new, right_new = lax.map(one_block, (gradient[expert], left_stat[expert][slot_of_block], right_stat[expert][slot_of_block]))
        update_list.append(precond)
        left_list.append(left_stat[expert].at[slot_of_block].set(left_new))
        right_list.append(right_stat[expert].at[slot_of_block].set(right_new))
    return (jnp.stack(update_list), jnp.stack(left_list), jnp.stack(right_list))
```

```python
import functools

import jax
import jax.numpy as jnp
from jax import lax
from jax.experimental import pallas as pl
from jax.experimental.pallas import tpu as pltpu
from jax.sharding import PartitionSpec as P

MESH = pl.DeviceIdType.MESH
F32 = jnp.float32
BF16 = jnp.bfloat16
NZ, NXC = 4, 8
HALF = 256

C0 = 25.0 / 16.0
C1 = -5.0 / 16.0 - 3125.0 / 4096.0
C2 = 3125.0 / 4096.0
C3 = -1250.0 / 4096.0
C4 = 250.0 / 4096.0
C5 = -25.0 / 4096.0
C6 = 1.0 / 4096.0


def split(value):
    high = value.astype(BF16)
    return high, (value - high.astype(F32)).astype(BF16)


def dot(a, b, dims=((1,), (0,))):
    return lax.dot_general(a, b, (dims, ((), ())), preferred_element_type=F32)


def total(value):
    return jnp.sum(jnp.sum(value, axis=1, keepdims=True), axis=0, keepdims=True)


def part(i):
    return pl.ds(i * HALF, HALF)


def body_kernel(
    assign_ref, slot_ref, grad_ref, left_ref, right_ref,
    update_ref, new_left_ref, new_right_ref,
    sent, m1, m2, held, back, n1, n2, returned,
    lbuf, rbuf, sums, sumv,
    sh, sl, a_buf, xh, xl, yh, yl, base, plh, pll, prh, prl,
    az_s, az_r, ax_s, ax_r, bz_s, bz_r, bx_s, bx_r, loc, sum_s, sum_r, io_in, io_out,
):
    e = lax.axis_index("expert")
    me = lax.axis_index("shard")
    z, xc = lax.div(me, NXC), lax.rem(me, NXC)

    def z_peer(d):
        return lax.rem(z + d, NZ)

    def xc_peer(d):
        return lax.rem(xc + d, NXC)

    barrier = pltpu.get_barrier_semaphore()
    for d in range(1, NZ):
        pl.semaphore_signal(barrier, inc=1, device_id=(e, z_peer(d) * NXC + xc), device_id_type=MESH)
        pl.semaphore_signal(barrier, inc=1, device_id=(lax.rem(e + d, 4), me), device_id_type=MESH)
    for d in range(1, NXC):
        pl.semaphore_signal(barrier, inc=1, device_id=(e, z * NXC + xc_peer(d)), device_id_type=MESH)

    loads = [
        pltpu.make_async_copy(left_ref.at[0], lbuf, io_in.at[0]),
        pltpu.make_async_copy(right_ref.at[0], rbuf, io_in.at[1]),
    ]
    for copy in loads:
        copy.start()

    def square_sum(b, acc):
        rows = grad_ref[0, b]
        sq = rows * rows
        for c in range(4):
            acc = acc + sq[0:8, c * 128:(c + 1) * 128] + sq[8:16, c * 128:(c + 1) * 128]
        return acc

    sums[0] = lax.fori_loop(0, grad_ref.shape[1], square_sum, jnp.zeros((8, 128), F32))

    def build(k):
        def one(d, carry):
            block = jnp.maximum(assign_ref[0, d * 3 + k], 0)
            sent[k, lax.div(d, NXC), lax.rem(d, NXC)] = grad_ref[0, block].reshape(2, 8, 512)
            return carry

        lax.fori_loop(0, NZ * NXC, one, 0)

    def a_copies(src, mid1, mid2, k, r):
        out = []
        for d in (1, 3, 2):
            t = z_peer(d)
            out.append(pltpu.make_async_remote_copy(
                src_ref=src.at[k, t, :, 0], dst_ref=mid1.at[k, z],
                send_sem=az_s.at[r, d - 1], recv_sem=az_r.at[r, d - 1],
                device_id=(e, t * NXC + xc), device_id_type=MESH))
        for d in (1, 7, 2, 6, 3, 5, 4):
            t = xc_peer(d)
            out.append(pltpu.make_async_remote_copy(
                src_ref=src.at[k, :, t, 1], dst_ref=mid2.at[k, xc],
                send_sem=ax_s.at[r, d - 1], recv_sem=ax_r.at[r, d - 1],
                device_id=(e, z * NXC + t), device_id_type=MESH))
        out.append(pltpu.make_async_copy(src.at[k, z, :, 0], mid1.at[k, z], loc.at[r, 0]))
        out.append(pltpu.make_async_copy(src.at[k, :, xc, 1], mid2.at[k, xc], loc.at[r, 1]))
        return out

    def b_copies(mid1, mid2, dst, k, r):
        out = []
        for d in (1, 7, 2, 6, 3, 5, 4):
            t = xc_peer(d)
            out.append(pltpu.make_async_remote_copy(
                src_ref=mid1.at[k, :, t], dst_ref=dst.at[k, :, xc, 0],
                send_sem=bx_s.at[r, d - 1], recv_sem=bx_r.at[r, d - 1],
                device_id=(e, z * NXC + t), device_id_type=MESH))
        for d in (1, 3, 2):
            t = z_peer(d)
            out.append(pltpu.make_async_remote_copy(
                src_ref=mid2.at[k, :, t], dst_ref=dst.at[k, z, :, 1],
                send_sem=bz_s.at[r, d - 1], recv_sem=bz_r.at[r, d - 1],
                device_id=(e, t * NXC + xc), device_id_type=MESH))
        out.append(pltpu.make_async_copy(mid1.at[k, :, xc], dst.at[k, :, xc, 0], loc.at[r, 2]))
        out.append(pltpu.make_async_copy(mid2.at[k, :, z], dst.at[k, z, :, 1], loc.at[r, 3]))
        return out

    def start(copies):
        for copy in copies:
            copy.start()

    def landed(copies):
        for copy in copies[:-2]:
            copy.wait_recv()
        for copy in copies[-2:]:
            copy.wait()

    def left_here(copies):
        for copy in copies[:-2]:
            copy.wait_send()

    fwd_a = lambda k: a_copies(sent, m1, m2, k, k)
    fwd_b = lambda k: b_copies(m1, m2, held, k, k)
    ret_a = lambda k: a_copies(back, n1, n2, k, 3 + k)
    ret_b = lambda k: b_copies(n1, n2, returned, k, 3 + k)

    build(0)
    pl.semaphore_wait(barrier, 2 * (NZ - 1) + NXC - 1)

    sum_copies = []

    def sum_stage(stage, first, peers):
        copies = []
        for i, peer in enumerate(peers):
            copies.append(pltpu.make_async_remote_copy(
                src_ref=sums.at[stage], dst_ref=sumv.at[first + i],
                send_sem=sum_s.at[first + i], recv_sem=sum_r.at[first + i],
                device_id=peer, device_id_type=MESH))
        start(copies)
        sum_copies.extend(copies)
        return copies

    def sum_take(stage, first, copies):
        acc = sums[stage]
        for i, copy in enumerate(copies):
            copy.wait_recv()
            acc = acc + sumv[first + i]
        sums[stage + 1] = acc

    s0 = sum_stage(0, 0, [(lax.rem(e + d, 4), me) for d in range(1, 4)])
    start(fwd_a(0))
    build(1)
    start(fwd_a(1))
    sum_take(0, 0, s0)
    s1 = sum_stage(1, 3, [(e, z_peer(d) * NXC + xc) for d in range(1, NZ)])
    build(2)
    sum_take(1, 3, s1)
    s2 = sum_stage(2, 6, [(e, z * NXC + xc_peer(d)) for d in range(1, NXC)])
    landed(fwd_a(0))
    start(fwd_b(0))
    sum_take(2, 6, s2)
    entries = 4.0 * 32.0 * 512.0 * 512.0
    mean_square = total(sums[3]) / entries
    factor = jnp.minimum(1.0, 1.0 / jnp.sqrt(mean_square + 1e-06))
    landed(fwd_a(1))
    start(fwd_b(1))
    start(fwd_a(2))
    for copy in loads:
        copy.wait()

    def put(high, low, i, j, value):
        a, b = split(value)
        high[part(i), part(j)] = a
        low[part(i), part(j)] = b

    def root(square, oh, ol):
        norm = jnp.sqrt(square + 1e-06)
        inverse = 1.0 / norm
        for i in range(2):
            for j in range(2):
                put(xh, xl, i, j, a_buf[part(i), part(j)] * inverse)
        for i, j in ((0, 0), (0, 1), (1, 1)):
            low = dot(xh[part(i), :], xl[:, part(j)])
            other = low if i == j else dot(xh[part(j), :], xl[:, part(i)])
            value = dot(xh[part(i), :], xh[:, part(j)]) + (low + other.T)
            put(yh, yl, i, j, value)
            base[part(i), part(j)] = value
            if i != j:
                put(yh, yl, j, i, value.T)
        cubes = {}
        for i, j in ((0, 0), (0, 1), (1, 1)):
            cubes[i, j] = (
                dot(yh[part(i), :], xh[:, part(j)])
                + (dot(yh[part(i), :], xl[:, part(j)]) + dot(yl[part(i), :], xh[:, part(j)]))
            )
            x1 = a_buf[part(i), part(j)] * inverse
            x2 = base[part(i), part(j)]
            x3 = cubes[i, j]
            value = C1 * x1 + C2 * x2 + C3 * x3
            if i == j:
                rows = lax.broadcasted_iota(jnp.int32, (HALF, HALF), 0)
                cols = lax.broadcasted_iota(jnp.int32, (HALF, HALF), 1)
                value = value + jnp.where(rows == cols, C0, 0.0)
            base[part(i), part(j)] = value
            a_buf[part(i), part(j)] = C4 * x1 + C5 * x2 + C6 * x3
            cubes[i, j] = None
            put(oh, ol, i, j, x3)
            if i != j:
                put(oh, ol, j, i, x3.T)
        for i, j in ((0, 0), (0, 1), (1, 1)):
            put(xh, xl, i, j, a_buf[part(i), part(j)])
            if i != j:
                put(xh, xl, j, i, a_buf[part(i), part(j)].T)
        for i, j in ((0, 0), (0, 1), (1, 1)):
            base[part(i), part(j)] += (
                dot(oh[part(i), :], xh[:, part(j)])
                + (dot(oh[part(i), :], xl[:, part(j)]) + dot(ol[part(i), :], xh[:, part(j)]))
            )
        for i, j in ((0, 0), (0, 1), (1, 1)):
            value = base[part(i), part(j)]
            put(oh, ol, i, j, value)
            if i != j:
                put(oh, ol, j, i, value.T)
        return jnp.sqrt(jnp.sqrt(norm))

    def stat(buf, k, live, products):
        square = jnp.zeros((1, 1), F32)
        for i in range(2):
            for j in range(2):
                old = buf[k, part(i), part(j)]
                new = 0.95 * old + products(i, j)
                a_buf[part(i), part(j)] = new
                square = square + total(new * new)
                buf[k, part(i), part(j)] = jnp.where(live, new, old)
        return square

    def slot(k):
        live = assign_ref[0, me * 3 + k] >= 0
        graft = jnp.zeros((1, 1), F32)
        for i in range(2):
            for j in range(2):
                piece = held[k, 2 * i:2 * i + 2, :, :, :, part(j)].reshape(HALF, HALF) * factor
                graft = graft + total(piece * piece)
                put(sh, sl, i, j, piece)

        def left_product(i, j):
            rows, cols = part(i), part(j)
            nt = ((1,), (1,))
            return dot(sh[rows, :], sh[cols, :], nt) + (
                dot(sh[rows, :], sl[cols, :], nt) + dot(sl[rows, :], sh[cols, :], nt))

        def right_product(i, j):
            rows, cols = part(i), part(j)
            tn = ((0,), (0,))
            return dot(sh[:, rows], sh[:, cols], tn) + (
                dot(sh[:, rows], sl[:, cols], tn) + dot(sl[:, rows], sh[:, cols], tn))

        left_scale = root(stat(lbuf, k, live, left_product), plh, pll)
        pltpu.make_async_copy(lbuf.at[k], new_left_ref.at[0, k], io_out.at[0, k]).start()
        right_scale = root(stat(rbuf, k, live, right_product), prh, prl)
        pltpu.make_async_copy(rbuf.at[k], new_right_ref.at[0, k], io_out.at[1, k]).start()

        for i in range(2):
            for j in range(2):
                put(xh, xl, i, j, dot(plh[part(i), :], sh[:, part(j)])
                    + (dot(plh[part(i), :], sl[:, part(j)]) + dot(pll[part(i), :], sh[:, part(j)])))
        square = jnp.zeros((1, 1), F32)
        scale = 1.0 / (left_scale * right_scale)
        for i in range(2):
            for j in range(2):
                value = dot(xh[part(i), :], prh[:, part(j)]) + (
                    dot(xh[part(i), :], prl[:, part(j)]) + dot(xl[part(i), :], prh[:, part(j)]))
                value = value * scale
                square = square + total(value * value)
                a_buf[part(i), part(j)] = value
        count = 512.0 * 512.0
        ratio = jnp.sqrt(graft / count + 1e-12) / jnp.sqrt(square / count + 1e-12)
        for i in range(2):
            back[k, 2 * i:2 * i + 2] = (a_buf[part(i), :] * ratio).reshape(2, NXC, 2, 8, 512)

    def turn(k, carry):
        landed(fwd_b(k))
        slot(k)
        start(ret_a(k))

        @pl.when(k == 0)
        def _():
            landed(fwd_a(2))
            start(fwd_b(2))

        @pl.when(k > 0)
        def _():
            landed(ret_a(k - 1))
            start(ret_b(k - 1))

        return carry

    lax.fori_loop(0, 3, turn, 0)
    landed(ret_a(2))
    start(ret_b(2))
    for k in range(3):
        left_here(fwd_a(k))
        left_here(fwd_b(k))
        left_here(ret_a(k))
    for copy in sum_copies:
        copy.wait_send()
    for k in range(3):
        pltpu.make_async_copy(lbuf.at[k], new_left_ref.at[0, k], io_out.at[0, k]).wait()
        pltpu.make_async_copy(rbuf.at[k], new_right_ref.at[0, k], io_out.at[1, k]).wait()
    for k in range(3):
        landed(ret_b(k))
        left_here(ret_b(k))

    def take(b, carry):
        s = slot_ref[0, b]
        d, k = lax.div(s, 3), lax.rem(s, 3)
        update_ref[0, b] = returned[k, lax.div(d, NXC), lax.rem(d, NXC)].reshape(16, 512)
        return carry

    lax.fori_loop(0, update_ref.shape[1], take, 0)


def body(gradient, left_stat, right_stat, assign):
    ids = jnp.arange(32, dtype=jnp.int32)
    slots = jnp.arange(96, dtype=jnp.int32)
    slot_of = jnp.sum(jnp.where(assign[0][None, :] == ids[:, None], slots[None, :], 0), axis=1).astype(jnp.int32)
    piece = (3, NZ, NXC, 2, 8, 512)
    vm = lambda shape, dtype=F32: pltpu.VMEM(shape, dtype)
    dma = lambda *shape: pltpu.SemaphoreType.DMA(shape)
    mat = (512, 512)
    any_spec = pl.BlockSpec(memory_space=pl.ANY)
    return pl.pallas_call(
        body_kernel,
        out_shape=(
            jax.ShapeDtypeStruct(gradient.shape, F32),
            jax.ShapeDtypeStruct(left_stat.shape, F32),
            jax.ShapeDtypeStruct(right_stat.shape, F32),
        ),
        in_specs=[
            pl.BlockSpec(memory_space=pltpu.SMEM),
            pl.BlockSpec(memory_space=pltpu.SMEM),
            pl.BlockSpec(memory_space=pltpu.VMEM),
            any_spec, any_spec,
        ],
        out_specs=(pl.BlockSpec(memory_space=pltpu.VMEM), any_spec, any_spec),
        scratch_shapes=[
            vm(piece), vm((3, NZ, NXC, 8, 512)), vm((3, NXC, NZ, 8, 512)), vm(piece),
            vm(piece), vm((3, NZ, NXC, 8, 512)), vm((3, NXC, NZ, 8, 512)), vm(piece),
            vm((3,) + mat), vm((3,) + mat), vm((4, 8, 128)), vm((13, 8, 128)),
            vm(mat, BF16), vm(mat, BF16), vm(mat), vm(mat, BF16), vm(mat, BF16), vm(mat, BF16), vm(mat, BF16), vm(mat),
            vm(mat, BF16), vm(mat, BF16), vm(mat, BF16), vm(mat, BF16),
            dma(6, 3), dma(6, 3), dma(6, 7), dma(6, 7), dma(6, 3), dma(6, 3), dma(6, 7), dma(6, 7),
            dma(6, 4), dma(13), dma(13), dma(2), dma(2, 3),
        ],
        name="shampoo",
        compiler_params=pltpu.CompilerParams(collective_id=0, has_side_effects=True, vmem_limit_bytes=58 * 2**20),
    )(assign, slot_of[None], gradient, left_stat, right_stat)


def solution(mesh):
    placed = P("expert", None, "shard", None)
    slots = P("expert", "shard", None, None)
    return jax.shard_map(
        body,
        mesh=mesh,
        in_specs=(placed, slots, slots, P("expert", None)),
        out_specs=(placed, slots, slots),
        check_vma=False,
    )
```

```python
import functools

import jax
import jax.numpy as jnp
from jax import lax
from jax.experimental import pallas as pl
from jax.experimental.pallas import tpu as pltpu
from jax.sharding import PartitionSpec as P

MESH = pl.DeviceIdType.MESH
F32 = jnp.float32
BF16 = jnp.bfloat16
HALF = 256
CAP = 8
FULL = 16
LIST_A, LIST_B, OWNER, ENTRY_A, ENTRY_B, OVER = range(6)

C0 = 25.0 / 16.0
C1 = -5.0 / 16.0 - 3125.0 / 4096.0
C2 = 3125.0 / 4096.0
C3 = -1250.0 / 4096.0
C4 = 250.0 / 4096.0
C5 = -25.0 / 4096.0
C6 = 1.0 / 4096.0


def split(value):
    high = value.astype(BF16)
    return high, (value - high.astype(F32)).astype(BF16)


def dot(a, b, dims=((1,), (0,))):
    return lax.dot_general(a, b, (dims, ((), ())), preferred_element_type=F32)


def total(value):
    return jnp.sum(jnp.sum(value, axis=1, keepdims=True), axis=0, keepdims=True)


def part(i):
    return pl.ds(i * HALF, HALF)


def place(slot):
    d = (slot * 43) >> 7
    z, x, c = d >> 3, (d >> 1) & 3, d & 1
    return slot - 3 * d, z, x, d & 7, z * 2 + c


def table_kernel(assign_ref, table_ref, row):
    shape = (128, 128)
    row[...] = jnp.full((8, 128), -1.0, F32)
    row[0:1, 0:96] = assign_ref[...].astype(F32)
    across = jnp.broadcast_to(row[0:1, :], shape)
    down = across.T
    i = lax.broadcasted_iota(jnp.int32, shape, 0)
    j = lax.broadcasted_iota(jnp.int32, shape, 1)
    rank_i, za_i, xa_i, _, _ = place(i)
    rank_j, za_j, xa_j, b0_j, b1_j = place(j)
    more_i = (down >= 0.0) & (rank_i > 0)
    more_j = (across >= 0.0) & (rank_j > 0)

    def count(mask, axis):
        return jnp.sum(jnp.where(mask, 1.0, 0.0), axis=axis, keepdims=True)

    over = jnp.zeros((1, 1), F32)
    for h, (ga_i, ga_j, b_j) in enumerate(((za_i, za_j, b0_j), (xa_i, xa_j, b1_j))):
        same = ga_i == ga_j
        before_i = count(more_j & same & (j < i), 1)
        before_j = count(more_i & same & (i < j), 0)
        listed = more_i & (ga_i == (j >> 4)) & (before_i == (j & 15).astype(F32))
        spots = jnp.sum(jnp.where(listed, i.astype(F32), 0.0), axis=0, keepdims=True)
        table_ref[LIST_A + h:LIST_A + h + 1, :] = spots.astype(jnp.int32)
        entry = jnp.where(rank_j[0:1] == 0, b_j[0:1].astype(F32), 8.0 + before_j)
        table_ref[ENTRY_A + h:ENTRY_A + h + 1, :] = entry.astype(jnp.int32)
        over = over + count(more_j[0:1] & (before_j >= float(CAP)), 1)
    owner = jnp.sum(jnp.where(down == j.astype(F32), i.astype(F32), 0.0), axis=0, keepdims=True)
    table_ref[OWNER:OWNER + 1, :] = owner.astype(jnp.int32)
    table_ref[OVER:OVER + 1, :] = jnp.broadcast_to(over, (1, 128)).astype(jnp.int32)
    table_ref[OVER + 1:8, :] = jnp.zeros((7 - OVER, 128), jnp.int32)


def step_kernel(
    cap,
    assign_ref, table_ref, grad_ref, left_ref, right_ref,
    update_ref, new_left_ref, new_right_ref, over_ref,
    sent, mid, pad, held, back, rmid, comp, fin,
    lbuf, rbuf, sums, sumv,
    sh, sl, a_buf, xh, xl, yh, yl, base, plh, pll, prh, prl,
    a_s, a_r, b_s, b_r, loc, sum_s, sum_r, io_in, io_out,
):
    e = lax.axis_index("expert")
    me = lax.axis_index("shard")
    z, x, c = lax.div(me, 8), lax.rem(lax.div(me, 2), 4), lax.rem(me, 2)
    group = (z, x)
    spot = (x * 2 + c, z * 2 + c)

    def device(h, a, b):
        if h == 0:
            return (e, a * 8 + b)
        return (e, lax.div(b, 2) * 8 + a * 2 + lax.rem(b, 2))

    def index(h, a, b):
        return device(h, a, b)[1]

    barrier = pltpu.get_barrier_semaphore()
    for d in range(1, 4):
        pl.semaphore_signal(barrier, inc=1, device_id=(lax.rem(e + d, 4), me), device_id_type=MESH)
    for d in range(1, 8):
        pl.semaphore_signal(barrier, inc=1, device_id=device(0, z, lax.rem(spot[0] + d, 8)), device_id_type=MESH)
    for d in range(1, 4):
        for f in range(2):
            pl.semaphore_signal(
                barrier, inc=1, device_id=(e, lax.rem(z + d, 4) * 8 + x * 2 + lax.rem(c + f, 2)), device_id_type=MESH)

    loads = [
        pltpu.make_async_copy(left_ref.at[0], lbuf, io_in.at[0]),
        pltpu.make_async_copy(right_ref.at[0], rbuf, io_in.at[1]),
    ]
    for copy in loads:
        copy.start()

    def square_sum(b, acc):
        rows = grad_ref[0, b]
        sq = rows * rows
        for q in range(4):
            acc = acc + sq[0:8, q * 128:(q + 1) * 128] + sq[8:16, q * 128:(q + 1) * 128]
        return acc

    sums[0, 0] = lax.fori_loop(0, grad_ref.shape[1], square_sum, jnp.zeros((8, 128), F32))
    sums[0, 1] = jnp.full((8, 128), table_ref[OVER, 0].astype(F32), F32)

    def build_first(d, carry):
        block = jnp.maximum(assign_ref[0, d * 3], 0)
        rows = grad_ref[0, block]
        zd, xd, cd = lax.div(d, 8), lax.rem(lax.div(d, 2), 4), lax.rem(d, 2)
        sent[0, zd, xd * 2 + cd] = rows[0:8]
        sent[1, xd, zd * 2 + cd] = rows[8:16]
        return carry

    def build_more(n, carry):
        a, j = lax.div(n, cap), lax.rem(n, cap)
        for h in range(2):
            block = jnp.maximum(assign_ref[0, table_ref[LIST_A + h, a * 16 + j]], 0)
            sent[h, a, 8 + j] = grad_ref[0, block, h * 8:h * 8 + 8]
        return carry

    def build_pad(k):
        def one(b, carry):
            for h in range(2):
                entry = jnp.minimum(table_ref[ENTRY_A + h, index(h, group[h], b) * 3 + k], 7 + cap)
                pad[k - 1, h, b] = mid[h, :, entry]
            return carry

        lax.fori_loop(0, 8, one, 0)

    def build_comp(j, carry):
        for h in range(2):
            rank, _, _, b0, b1 = place(table_ref[LIST_A + h, group[h] * 16 + j])
            comp[h, :, j] = rmid[rank, h, (b0, b1)[h]]
        return carry

    first, more = pl.ds(0, 8), pl.ds(8, cap)
    near, ring = (1, 3, 2), (1, 7, 2, 6, 3, 5, 4)

    def along(r, src, dst):
        out, here = [], []
        for d in near:
            for h in range(2):
                t = lax.rem(group[h] + d, 4)
                out.append(pltpu.make_async_remote_copy(
                    src_ref=src(h, t), dst_ref=dst(h, group[h]),
                    send_sem=a_s.at[r, h, d - 1], recv_sem=a_r.at[r, h, d - 1],
                    device_id=device(h, t, spot[h]), device_id_type=MESH))
        for h in range(2):
            here.append(pltpu.make_async_copy(src(h, group[h]), dst(h, group[h]), loc.at[r, h]))
        return out, here

    def within(r, src, dst):
        out, here = [], []
        for d in ring:
            for h in range(2):
                t = lax.rem(spot[h] + d, 8)
                out.append(pltpu.make_async_remote_copy(
                    src_ref=src(h, t), dst_ref=dst(h, spot[h]),
                    send_sem=b_s.at[r, h, d - 1], recv_sem=b_r.at[r, h, d - 1],
                    device_id=device(h, group[h], t), device_id_type=MESH))
        for h in range(2):
            here.append(pltpu.make_async_copy(src(h, spot[h]), dst(h, spot[h]), loc.at[4 + r, h]))
        return out, here

    def rows_of(ref, k):
        def pick(h, b):
            if h == 0:
                return ref.at[k, :, lax.div(b, 2), lax.rem(b, 2), 0]
            return ref.at[k, lax.div(b, 2), :, lax.rem(b, 2), 1]

        return pick

    out_first = lambda: along(0, lambda h, a: sent.at[h, a, first], lambda h, a: mid.at[h, a, first])
    out_more = lambda: along(1, lambda h, a: sent.at[h, a, more], lambda h, a: mid.at[h, a, more])
    to_first = lambda: within(0, lambda h, b: mid.at[h, :, b], rows_of(held, 0))
    to_more = lambda k: within(k, lambda h, b: pad.at[k - 1, h, b], rows_of(held, k))
    arrive = lambda k: within(k, lambda h, b: pad.at[0, h, b], rows_of(held, k))
    from_slot = lambda k: within(3 + k, rows_of(back, k), lambda h, b: rmid.at[k, h, b])
    in_first = lambda: along(2, lambda h, a: rmid.at[0, h, :, a], lambda h, a: fin.at[h, a, first])
    in_more = lambda: along(3, lambda h, a: comp.at[h, a], lambda h, a: fin.at[h, a, more])

    def start(copies):
        for copy in copies[0] + copies[1]:
            copy.start()

    def landed(copies):
        for copy in copies[0]:
            copy.wait_recv()
        for copy in copies[1]:
            copy.wait()

    def gone(copies):
        for copy in copies[0]:
            copy.wait_send()

    lax.fori_loop(0, 32, build_first, 0)
    pl.semaphore_wait(barrier, 16)

    sum_copies = []

    def sum_stage(stage, at, peers):
        copies = []
        for i, peer in enumerate(peers):
            copies.append(pltpu.make_async_remote_copy(
                src_ref=sums.at[stage], dst_ref=sumv.at[at + i],
                send_sem=sum_s.at[at + i], recv_sem=sum_r.at[at + i],
                device_id=peer, device_id_type=MESH))
        for copy in copies:
            copy.start()
        sum_copies.extend(copies)
        return copies

    def sum_take(stage, at, copies):
        acc = sums[stage]
        for i, copy in enumerate(copies):
            copy.wait_recv()
            acc = acc + sumv[at + i]
        sums[stage + 1] = acc

    s0 = sum_stage(0, 0, [(lax.rem(e + d, 4), me) for d in range(1, 4)])
    start(out_first())
    lax.fori_loop(0, 4 * cap, build_more, 0)
    start(out_more())
    sum_take(0, 0, s0)
    s1 = sum_stage(1, 3, [device(0, lax.rem(z + d, 4), spot[0]) for d in range(1, 4)])
    sum_take(1, 3, s1)
    s2 = sum_stage(2, 6, [device(0, z, lax.rem(spot[0] + d, 8)) for d in range(1, 8)])
    landed(out_first())
    start(to_first())
    sum_take(2, 6, s2)
    mean_square = total(sums[3, 0]) / (4.0 * 32.0 * 512.0 * 512.0)
    factor = jnp.minimum(1.0, 1.0 / jnp.sqrt(mean_square + 1e-06))
    over_ref[...] = sums[3, 1]
    landed(out_more())
    build_pad(1)
    start(to_more(1))
    build_pad(2)
    start(to_more(2))
    for copy in loads:
        copy.wait()

    def put(high, low, i, j, value):
        a, b = split(value)
        high[part(i), part(j)] = a
        low[part(i), part(j)] = b

    def both(high, low, i, j, value):
        put(high, low, i, j, value)
        if i != j:
            put(high, low, j, i, value.T)

    tiles = ((0, 0), (0, 1), (1, 1))

    def root(square, oh, ol):
        norm = jnp.sqrt(square + 1e-06)
        inverse = 1.0 / norm
        for i in range(2):
            for j in range(2):
                put(xh, xl, i, j, a_buf[part(i), part(j)] * inverse)
        for i, j in tiles:
            low = dot(xh[part(i), :], xl[:, part(j)])
            other = low if i == j else dot(xh[part(j), :], xl[:, part(i)])
            value = dot(xh[part(i), :], xh[:, part(j)]) + (low + other.T)
            both(yh, yl, i, j, value)
            base[part(i), part(j)] = value
        for i, j in tiles:
            x3 = (
                dot(yh[part(i), :], xh[:, part(j)])
                + (dot(yh[part(i), :], xl[:, part(j)]) + dot(yl[part(i), :], xh[:, part(j)]))
            )
            x1 = a_buf[part(i), part(j)] * inverse
            x2 = base[part(i), part(j)]
            value = C1 * x1 + C2 * x2 + C3 * x3
            if i == j:
                rows = lax.broadcasted_iota(jnp.int32, (HALF, HALF), 0)
                cols = lax.broadcasted_iota(jnp.int32, (HALF, HALF), 1)
                value = value + jnp.where(rows == cols, C0, 0.0)
            base[part(i), part(j)] = value
            high = x3.astype(BF16)
            rest = (C4 * x1 + C5 * x2 + C6 * x3)
            oh[part(i), part(j)] = high
            ol[part(i), part(j)] = rest.astype(BF16)
            if i != j:
                oh[part(j), part(i)] = x3.T.astype(BF16)
                ol[part(j), part(i)] = rest.T.astype(BF16)
        for i, j in tiles:
            base[part(i), part(j)] += dot(oh[part(i), :], ol[:, part(j)])
        for i, j in tiles:
            both(oh, ol, i, j, base[part(i), part(j)])
        return jnp.sqrt(jnp.sqrt(norm))

    def stat(buf, k, live, high, low):
        square = jnp.zeros((1, 1), F32)

        def take(i, j, product):
            old = buf[k, part(i), part(j)]
            new = 0.95 * old + product
            a_buf[part(i), part(j)] = new
            buf[k, part(i), part(j)] = jnp.where(live, new, old)
            return total(new * new)

        for i, j in tiles:
            one = low(i, j)
            other = one if i == j else low(j, i)
            product = high(i, j) + (one + other.T)
            square = square + take(i, j, product)
            if i != j:
                square = square + take(j, i, product.T)
        return square

    def slot(k):
        live = assign_ref[0, me * 3 + k] >= 0
        graft = jnp.zeros((1, 1), F32)
        for i in range(2):
            for j in range(2):
                piece = held[k, 2 * i:2 * i + 2, :, :, :, :, part(j)].reshape(HALF, HALF) * factor
                graft = graft + total(piece * piece)
                put(sh, sl, i, j, piece)
        nt, tn = ((1,), (1,)), ((0,), (0,))
        left_scale = root(stat(
            lbuf, k, live,
            lambda i, j: dot(sh[part(i), :], sh[part(j), :], nt),
            lambda i, j: dot(sh[part(i), :], sl[part(j), :], nt)), plh, pll)
        pltpu.make_async_copy(lbuf.at[k], new_left_ref.at[0, k], io_out.at[0, k]).start()
        right_scale = root(stat(
            rbuf, k, live,
            lambda i, j: dot(sh[:, part(i)], sh[:, part(j)], tn),
            lambda i, j: dot(sh[:, part(i)], sl[:, part(j)], tn)), prh, prl)
        pltpu.make_async_copy(rbuf.at[k], new_right_ref.at[0, k], io_out.at[1, k]).start()

        for i in range(2):
            for j in range(2):
                put(xh, xl, i, j, dot(plh[part(i), :], sh[:, part(j)])
                    + (dot(plh[part(i), :], sl[:, part(j)]) + dot(pll[part(i), :], sh[:, part(j)])))
        square = jnp.zeros((1, 1), F32)
        scale = 1.0 / (left_scale * right_scale)
        for i in range(2):
            for j in range(2):
                value = dot(xh[part(i), :], prh[:, part(j)]) + (
                    dot(xh[part(i), :], prl[:, part(j)]) + dot(xl[part(i), :], prh[:, part(j)]))
                value = value * scale
                square = square + total(value * value)
                a_buf[part(i), part(j)] = value
        count = 512.0 * 512.0
        ratio = jnp.sqrt(graft / count + 1e-12) / jnp.sqrt(square / count + 1e-12)
        for i in range(2):
            back[k, 2 * i:2 * i + 2] = (a_buf[part(i), :] * ratio).reshape(2, 4, 2, 2, 8, 512)

    def turn(k, carry):
        landed(arrive(k))
        slot(k)
        start(from_slot(k))

        @pl.when(k == 1)
        def _():
            landed(from_slot(0))
            start(in_first())

        return carry

    lax.fori_loop(0, 3, turn, 0)
    landed(from_slot(1))
    landed(from_slot(2))
    lax.fori_loop(0, cap, build_comp, 0)
    start(in_more())
    gone(out_first())
    gone(out_more())
    gone(to_first())
    gone(to_more(1))
    gone(to_more(2))
    for k in range(3):
        gone(from_slot(k))
    for copy in sum_copies:
        copy.wait_send()
    for k in range(3):
        pltpu.make_async_copy(lbuf.at[k], new_left_ref.at[0, k], io_out.at[0, k]).wait()
        pltpu.make_async_copy(rbuf.at[k], new_right_ref.at[0, k], io_out.at[1, k]).wait()
    for copies in (in_first(), in_more()):
        landed(copies)
        gone(copies)

    def take(b, carry):
        s = table_ref[OWNER, b]
        _, za, xa, _, _ = place(s)
        for h, a in enumerate((za, xa)):
            entry = jnp.minimum(table_ref[ENTRY_A + h, s], 7 + cap)
            update_ref[0, b, h * 8:h * 8 + 8] = fin[h, a, entry]
        return carry

    lax.fori_loop(0, update_ref.shape[1], take, 0)


def step(cap, ident, assign, table, gradient, left_stat, right_stat):
    vm = lambda *shape, dtype=F32: pltpu.VMEM(shape, dtype)
    half = lambda *shape: pltpu.VMEM(shape, BF16)
    dma = lambda *shape: pltpu.SemaphoreType.DMA(shape)
    any_spec = pl.BlockSpec(memory_space=pl.ANY)
    smem = pl.BlockSpec(memory_space=pltpu.SMEM)
    vmem = pl.BlockSpec(memory_space=pltpu.VMEM)
    entries = 8 + cap
    piece = (3, 4, 4, 2, 2, 8, 512)
    return pl.pallas_call(
        functools.partial(step_kernel, cap),
        out_shape=(
            jax.ShapeDtypeStruct(gradient.shape, F32),
            jax.ShapeDtypeStruct(left_stat.shape, F32),
            jax.ShapeDtypeStruct(right_stat.shape, F32),
            jax.ShapeDtypeStruct((8, 128), F32),
        ),
        in_specs=[smem, smem, vmem, any_spec, any_spec],
        out_specs=(vmem, any_spec, any_spec, vmem),
        scratch_shapes=[
            vm(2, 4, entries, 8, 512), vm(2, 4, entries, 8, 512), vm(2, 2, 8, 4, 8, 512), vm(*piece),
            vm(*piece), vm(3, 2, 8, 4, 8, 512), vm(2, 4, cap, 8, 512), vm(2, 4, entries, 8, 512),
            vm(3, 512, 512), vm(3, 512, 512), vm(4, 2, 8, 128), vm(13, 2, 8, 128),
            half(512, 512), half(512, 512), vm(512, 512), half(512, 512), half(512, 512), half(512, 512),
            half(512, 512), vm(512, 512), half(512, 512), half(512, 512), half(512, 512), half(512, 512),
            dma(4, 2, 3), dma(4, 2, 3), dma(6, 2, 7), dma(6, 2, 7), dma(10, 2), dma(13), dma(13), dma(2), dma(2, 3),
        ],
        name="step" + str(cap),
        compiler_params=pltpu.CompilerParams(collective_id=ident, has_side_effects=True, vmem_limit_bytes=58 * 2**20),
    )(assign, table, gradient, left_stat, right_stat)


def body(gradient, left_stat, right_stat, assign):
    table = pl.pallas_call(
        table_kernel,
        out_shape=jax.ShapeDtypeStruct((8, 128), jnp.int32),
        in_specs=[pl.BlockSpec(memory_space=pltpu.VMEM)],
        out_specs=pl.BlockSpec(memory_space=pltpu.VMEM),
        scratch_shapes=[pltpu.VMEM((8, 128), F32)],
        name="table",
    )(assign)
    *outs, over = step(CAP, 0, assign, table, gradient, left_stat, right_stat)

    def again(_):
        return tuple(step(FULL, 1, assign, table, gradient, left_stat, right_stat)[:3])

    return lax.cond(over[0, 0] > 0.0, again, lambda kept: kept, tuple(outs))


def solution(mesh):
    placed = P("expert", None, "shard", None)
    slots = P("expert", "shard", None, None)
    return jax.shard_map(
        body,
        mesh=mesh,
        in_specs=(placed, slots, slots, P("expert", None)),
        out_specs=(placed, slots, slots),
        check_vma=False,
    )
```

```python
import functools

import jax
import jax.numpy as jnp
from jax import lax
from jax.experimental import pallas as pl
from jax.experimental.pallas import tpu as pltpu
from jax.sharding import PartitionSpec as P

MESH = pl.DeviceIdType.MESH
F32 = jnp.float32
BF16 = jnp.bfloat16
HALF = 256
CAP = 8
FULL = 16
LIST_A, LIST_B, OWNER, ENTRY_A, ENTRY_B, OVER = range(6)

C0 = 25.0 / 16.0
C1 = -5.0 / 16.0 - 3125.0 / 4096.0
C2 = 3125.0 / 4096.0
C3 = -1250.0 / 4096.0
C4 = 250.0 / 4096.0
C5 = -25.0 / 4096.0
C6 = 1.0 / 4096.0


def split(value):
    high = value.astype(BF16)
    return high, (value - high.astype(F32)).astype(BF16)


def dot(a, b, dims=((1,), (0,))):
    return lax.dot_general(a, b, (dims, ((), ())), preferred_element_type=F32)


def total(value):
    return jnp.sum(jnp.sum(value, axis=1, keepdims=True), axis=0, keepdims=True)


def part(i):
    return pl.ds(i * HALF, HALF)


def place(slot):
    d = (slot * 43) >> 7
    z, x, c = d >> 3, (d >> 1) & 3, d & 1
    return slot - 3 * d, z, x, d & 7, z * 2 + c


def fill_table(assign_ref, table_ref, row):
    shape = (128, 128)
    row[...] = jnp.full((8, 128), -1.0, F32)
    row[0:1, 0:96] = assign_ref[...].astype(F32)
    across = jnp.broadcast_to(row[0:1, :], shape)
    down = across.T
    i = lax.broadcasted_iota(jnp.int32, shape, 0)
    j = lax.broadcasted_iota(jnp.int32, shape, 1)
    rank_i, za_i, xa_i, _, _ = place(i)
    rank_j, za_j, xa_j, b0_j, b1_j = place(j)
    more_i = (down >= 0.0) & (rank_i > 0)
    more_j = (across >= 0.0) & (rank_j > 0)

    def count(mask, axis):
        return jnp.sum(jnp.where(mask, 1.0, 0.0), axis=axis, keepdims=True)

    over = jnp.zeros((1, 1), F32)
    for h, (ga_i, ga_j, b_j) in enumerate(((za_i, za_j, b0_j), (xa_i, xa_j, b1_j))):
        same = ga_i == ga_j
        before_i = count(more_j & same & (j < i), 1)
        before_j = count(more_i & same & (i < j), 0)
        listed = more_i & (ga_i == (j >> 4)) & (before_i == (j & 15).astype(F32))
        spots = jnp.sum(jnp.where(listed, i.astype(F32), 0.0), axis=0, keepdims=True)
        table_ref[LIST_A + h:LIST_A + h + 1, :] = jnp.minimum(spots, 95.0).astype(jnp.int32)
        entry = jnp.where(rank_j[0:1] == 0, b_j[0:1].astype(F32), 8.0 + before_j)
        table_ref[ENTRY_A + h:ENTRY_A + h + 1, :] = jnp.clip(entry, 0.0, 23.0).astype(jnp.int32)
        over = over + count(more_j[0:1] & (before_j >= float(CAP)), 1)
    owner = jnp.sum(jnp.where(down == j.astype(F32), i.astype(F32), 0.0), axis=0, keepdims=True)
    table_ref[OWNER:OWNER + 1, :] = jnp.minimum(owner, 95.0).astype(jnp.int32)
    table_ref[OVER:OVER + 1, :] = jnp.broadcast_to(over, (1, 128)).astype(jnp.int32)
    table_ref[OVER + 1:8, :] = jnp.zeros((7 - OVER, 128), jnp.int32)


def step_kernel(
    cap,
    assign_ref, row_ref, gradient_ref, left_ref, right_ref,
    update_ref, new_left_ref, new_right_ref, over_ref,
    sent, mid, pad, held, back, rmid, comp, fin,
    grad_ref, lbuf, rbuf, sums, sumv, sumy, row, table_v, table_ref,
    sh, sl, a_buf, xh, xl, yh, yl, base, plh, pll, prh, prl,
    a_s, a_r, b_s, b_r, loc, sum_s, sum_r, y_s, y_r, io_in, io_out,
):
    e = lax.axis_index("expert")
    me = lax.axis_index("shard")
    z, x, c = lax.div(me, 8), lax.rem(lax.div(me, 2), 4), lax.rem(me, 2)
    group = (z, x)
    spot = (x * 2 + c, z * 2 + c)

    def device(h, a, b):
        if h == 0:
            return (e, a * 8 + b)
        return (e, lax.div(b, 2) * 8 + a * 2 + lax.rem(b, 2))

    def index(h, a, b):
        return device(h, a, b)[1]

    barrier = pltpu.get_barrier_semaphore()
    for d in range(1, 4):
        pl.semaphore_signal(barrier, inc=1, device_id=(lax.rem(e + d, 4), me), device_id_type=MESH)
    for d in range(1, 32):
        pl.semaphore_signal(barrier, inc=1, device_id=(e, lax.rem(me + d, 32)), device_id_type=MESH)

    fetch = pltpu.make_async_copy(gradient_ref, grad_ref, io_in.at[2])
    fetch.start()
    loads = [
        pltpu.make_async_copy(left_ref.at[0], lbuf, io_in.at[0]),
        pltpu.make_async_copy(right_ref.at[0], rbuf, io_in.at[1]),
    ]
    for copy in loads:
        copy.start()
    fill_table(row_ref, table_v, row)
    lists = pltpu.make_async_copy(table_v, table_ref, io_in.at[3])
    lists.start()

    def square_sum(b, acc):
        rows = grad_ref[0, b]
        sq = rows * rows
        for q in range(4):
            acc = acc + sq[0:8, q * 128:(q + 1) * 128] + sq[8:16, q * 128:(q + 1) * 128]
        return acc

    fetch.wait()
    squares = lax.fori_loop(0, grad_ref.shape[1], square_sum, jnp.zeros((8, 128), F32))
    sums[...] = jnp.sum(squares, axis=0, keepdims=True)

    def look(line, at, top):
        return jnp.clip(table_ref[line, at], 0, top)

    def build_first(d, carry):
        block = jnp.clip(assign_ref[0, d * 3], 0, 31)
        rows = grad_ref[0, block]
        zd, xd, cd = lax.div(d, 8), lax.rem(lax.div(d, 2), 4), lax.rem(d, 2)
        sent[0, zd, xd * 2 + cd] = rows[0:8]
        sent[1, xd, zd * 2 + cd] = rows[8:16]
        return carry

    def build_more(n, carry):
        a, j = lax.div(n, cap), lax.rem(n, cap)
        for h in range(2):
            block = jnp.clip(assign_ref[0, look(LIST_A + h, a * 16 + j, 95)], 0, 31)
            sent[h, a, 8 + j] = grad_ref[0, block, h * 8:h * 8 + 8]
        return carry

    def build_pad(k):
        def one(b, carry):
            for h in range(2):
                entry = look(ENTRY_A + h, index(h, group[h], b) * 3 + k, 7 + cap)
                pad[k - 1, h, b] = mid[h, :, entry]
            return carry

        lax.fori_loop(0, 8, one, 0)

    def build_comp(j, carry):
        for h in range(2):
            rank, _, _, b0, b1 = place(look(LIST_A + h, group[h] * 16 + j, 95))
            comp[h, :, j] = rmid[rank, h, (b0, b1)[h]]
        return carry

    first, more = pl.ds(0, 8), pl.ds(8, cap)
    near, ring = (1, 3, 2), (1, 7, 2, 6, 3, 5, 4)

    def along(r, src, dst):
        out, here = [], []
        for d in near:
            for h in range(2):
                t = lax.rem(group[h] + d, 4)
                out.append(pltpu.make_async_remote_copy(
                    src_ref=src(h, t), dst_ref=dst(h, group[h]),
                    send_sem=a_s.at[r, h, d - 1], recv_sem=a_r.at[r, h, d - 1],
                    device_id=device(h, t, spot[h]), device_id_type=MESH))
        for h in range(2):
            here.append(pltpu.make_async_copy(src(h, group[h]), dst(h, group[h]), loc.at[r, h]))
        return out, here

    def within(r, src, dst):
        out, here = [], []
        for d in ring:
            for h in range(2):
                t = lax.rem(spot[h] + d, 8)
                out.append(pltpu.make_async_remote_copy(
                    src_ref=src(h, t), dst_ref=dst(h, spot[h]),
                    send_sem=b_s.at[r, h, d - 1], recv_sem=b_r.at[r, h, d - 1],
                    device_id=device(h, group[h], t), device_id_type=MESH))
        for h in range(2):
            here.append(pltpu.make_async_copy(src(h, spot[h]), dst(h, spot[h]), loc.at[4 + r, h]))
        return out, here

    def rows_of(ref, k):
        def pick(h, b):
            if h == 0:
                return ref.at[k, :, lax.div(b, 2), lax.rem(b, 2), 0]
            return ref.at[k, lax.div(b, 2), :, lax.rem(b, 2), 1]

        return pick

    out_first = lambda: along(0, lambda h, a: sent.at[h, a, first], lambda h, a: mid.at[h, a, first])
    out_more = lambda: along(1, lambda h, a: sent.at[h, a, more], lambda h, a: mid.at[h, a, more])
    to_first = lambda: within(0, lambda h, b: mid.at[h, :, b], rows_of(held, 0))
    to_more = lambda k: within(k, lambda h, b: pad.at[k - 1, h, b], rows_of(held, k))
    arrive = lambda k: within(k, lambda h, b: pad.at[0, h, b], rows_of(held, k))
    from_slot = lambda k: within(3 + k, rows_of(back, k), lambda h, b: rmid.at[k, h, b])
    in_first = lambda: along(2, lambda h, a: rmid.at[0, h, :, a], lambda h, a: fin.at[h, a, first])
    in_more = lambda: along(3, lambda h, a: comp.at[h, a], lambda h, a: fin.at[h, a, more])

    def start(copies):
        for copy in copies[0] + copies[1]:
            copy.start()

    def landed(copies):
        for copy in copies[0]:
            copy.wait_recv()
        for copy in copies[1]:
            copy.wait()

    def gone(copies):
        for copy in copies[0]:
            copy.wait_send()

    lax.fori_loop(0, 32, build_first, 0)
    lists.wait()
    lax.fori_loop(0, 4 * cap, build_more, 0)
    pl.semaphore_wait(barrier, 34)

    sum_copies = []
    for d in range(1, 32):
        sum_copies.append(pltpu.make_async_remote_copy(
            src_ref=sums, dst_ref=sumv.at[d - 1], send_sem=sum_s.at[d - 1], recv_sem=sum_r.at[d - 1],
            device_id=(e, lax.rem(me + d, 32)), device_id_type=MESH))
    for copy in sum_copies:
        copy.start()
    start(out_first())
    start(out_more())
    acc = sums[...]
    for d, copy in enumerate(sum_copies):
        copy.wait_recv()
        acc = acc + sumv[d]
    sumy[0, 0:1, :] = acc
    sumy[0, 1:2, :] = jnp.full((1, 128), table_ref[OVER, 0].astype(F32), F32)
    sumy[0, 2:8, :] = jnp.zeros((6, 128), F32)
    y_copies = []
    for d in range(1, 4):
        y_copies.append(pltpu.make_async_remote_copy(
            src_ref=sumy.at[0], dst_ref=sumy.at[d], send_sem=y_s.at[d - 1], recv_sem=y_r.at[d - 1],
            device_id=(lax.rem(e + d, 4), me), device_id_type=MESH))
    for copy in y_copies:
        copy.start()
    landed(out_first())
    start(to_first())
    acc = sumy[0]
    for d, copy in enumerate(y_copies):
        copy.wait_recv()
        acc = acc + sumy[d + 1]
    mean_square = total(acc[0:1, :]) / (4.0 * 32.0 * 512.0 * 512.0)
    factor = jnp.minimum(1.0, 1.0 / jnp.sqrt(mean_square + 1e-06))
    over_ref[...] = acc
    landed(out_more())
    build_pad(1)
    start(to_more(1))
    build_pad(2)
    start(to_more(2))
    for copy in loads:
        copy.wait()

    def put(high, low, i, j, value):
        a, b = split(value)
        high[part(i), part(j)] = a
        low[part(i), part(j)] = b

    def both(high, low, i, j, value):
        put(high, low, i, j, value)
        if i != j:
            put(high, low, j, i, value.T)

    tiles = ((0, 0), (0, 1), (1, 1))

    def root(square, oh, ol):
        norm = jnp.sqrt(square + 1e-06)
        inverse = 1.0 / norm
        for i in range(2):
            for j in range(2):
                put(xh, xl, i, j, a_buf[part(i), part(j)] * inverse)
        for i, j in tiles:
            low = dot(xh[part(i), :], xl[:, part(j)])
            other = low if i == j else dot(xh[part(j), :], xl[:, part(i)])
            value = dot(xh[part(i), :], xh[:, part(j)]) + (low + other.T)
            both(yh, yl, i, j, value)
            base[part(i), part(j)] = value
        for i, j in tiles:
            x3 = (
                dot(yh[part(i), :], xh[:, part(j)])
                + (dot(yh[part(i), :], xl[:, part(j)]) + dot(yl[part(i), :], xh[:, part(j)]))
            )
            x1 = a_buf[part(i), part(j)] * inverse
            x2 = base[part(i), part(j)]
            value = C1 * x1 + C2 * x2 + C3 * x3
            if i == j:
                rows = lax.broadcasted_iota(jnp.int32, (HALF, HALF), 0)
                cols = lax.broadcasted_iota(jnp.int32, (HALF, HALF), 1)
                value = value + jnp.where(rows == cols, C0, 0.0)
            base[part(i), part(j)] = value
            high = x3.astype(BF16)
            rest = (C4 * x1 + C5 * x2 + C6 * x3)
            oh[part(i), part(j)] = high
            ol[part(i), part(j)] = rest.astype(BF16)
            if i != j:
                oh[part(j), part(i)] = x3.T.astype(BF16)
                ol[part(j), part(i)] = rest.T.astype(BF16)
        for i, j in tiles:
            base[part(i), part(j)] += dot(oh[part(i), :], ol[:, part(j)])
        for i, j in tiles:
            both(oh, ol, i, j, base[part(i), part(j)])
        return jnp.sqrt(jnp.sqrt(norm))

    def stat(buf, k, live, high, low):
        square = jnp.zeros((1, 1), F32)

        def take(i, j, product):
            old = buf[k, part(i), part(j)]
            new = 0.95 * old + product
            a_buf[part(i), part(j)] = new
            buf[k, part(i), part(j)] = jnp.where(live, new, old)
            return total(new * new)

        for i, j in tiles:
            one = low(i, j)
            other = one if i == j else low(j, i)
            product = high(i, j) + (one + other.T)
            square = square + take(i, j, product)
            if i != j:
                square = square + take(j, i, product.T)
        return square

    def slot(k):
        live = assign_ref[0, me * 3 + k] >= 0
        graft = jnp.zeros((1, 1), F32)
        for i in range(2):
            for j in range(2):
                piece = held[k, 2 * i:2 * i + 2, :, :, :, :, part(j)].reshape(HALF, HALF) * factor
                graft = graft + total(piece * piece)
                put(sh, sl, i, j, piece)
        nt, tn = ((1,), (1,)), ((0,), (0,))
        left_scale = root(stat(
            lbuf, k, live,
            lambda i, j: dot(sh[part(i), :], sh[part(j), :], nt),
            lambda i, j: dot(sh[part(i), :], sl[part(j), :], nt)), plh, pll)
        pltpu.make_async_copy(lbuf.at[k], new_left_ref.at[0, k], io_out.at[0, k]).start()
        right_scale = root(stat(
            rbuf, k, live,
            lambda i, j: dot(sh[:, part(i)], sh[:, part(j)], tn),
            lambda i, j: dot(sh[:, part(i)], sl[:, part(j)], tn)), prh, prl)
        pltpu.make_async_copy(rbuf.at[k], new_right_ref.at[0, k], io_out.at[1, k]).start()

        for i in range(2):
            for j in range(2):
                put(xh, xl, i, j, dot(plh[part(i), :], sh[:, part(j)])
                    + (dot(plh[part(i), :], sl[:, part(j)]) + dot(pll[part(i), :], sh[:, part(j)])))
        square = jnp.zeros((1, 1), F32)
        scale = 1.0 / (left_scale * right_scale)
        for i in range(2):
            for j in range(2):
                value = dot(xh[part(i), :], prh[:, part(j)]) + (
                    dot(xh[part(i), :], prl[:, part(j)]) + dot(xl[part(i), :], prh[:, part(j)]))
                value = value * scale
                square = square + total(value * value)
                a_buf[part(i), part(j)] = value
        count = 512.0 * 512.0
        ratio = jnp.sqrt(graft / count + 1e-12) / jnp.sqrt(square / count + 1e-12)
        for i in range(2):
            back[k, 2 * i:2 * i + 2] = (a_buf[part(i), :] * ratio).reshape(2, 4, 2, 2, 8, 512)

    def turn(k, carry):
        landed(arrive(k))
        slot(k)
        start(from_slot(k))

        @pl.when(k == 1)
        def _():
            landed(from_slot(0))
            start(in_first())

        return carry

    lax.fori_loop(0, 3, turn, 0)
    landed(from_slot(1))
    landed(from_slot(2))
    lax.fori_loop(0, cap, build_comp, 0)
    start(in_more())
    gone(out_first())
    gone(out_more())
    gone(to_first())
    gone(to_more(1))
    gone(to_more(2))
    for k in range(3):
        gone(from_slot(k))
    for copy in sum_copies + y_copies:
        copy.wait_send()
    for k in range(3):
        pltpu.make_async_copy(lbuf.at[k], new_left_ref.at[0, k], io_out.at[0, k]).wait()
        pltpu.make_async_copy(rbuf.at[k], new_right_ref.at[0, k], io_out.at[1, k]).wait()
    for copies in (in_first(), in_more()):
        landed(copies)
        gone(copies)

    def take(b, carry):
        s = look(OWNER, b, 95)
        _, za, xa, _, _ = place(s)
        for h, a in enumerate((za, xa)):
            entry = look(ENTRY_A + h, s, 7 + cap)
            update_ref[0, b, h * 8:h * 8 + 8] = fin[h, a, entry]
        return carry

    lax.fori_loop(0, update_ref.shape[1], take, 0)


def step(cap, ident, assign, gradient, left_stat, right_stat):
    vm = lambda *shape, dtype=F32: pltpu.VMEM(shape, dtype)
    half = lambda *shape: pltpu.VMEM(shape, BF16)
    dma = lambda *shape: pltpu.SemaphoreType.DMA(shape)
    any_spec = pl.BlockSpec(memory_space=pl.ANY)
    smem = pl.BlockSpec(memory_space=pltpu.SMEM)
    vmem = pl.BlockSpec(memory_space=pltpu.VMEM)
    entries = 8 + cap
    piece = (3, 4, 4, 2, 2, 8, 512)
    return pl.pallas_call(
        functools.partial(step_kernel, cap),
        out_shape=(
            jax.ShapeDtypeStruct(gradient.shape, F32),
            jax.ShapeDtypeStruct(left_stat.shape, F32),
            jax.ShapeDtypeStruct(right_stat.shape, F32),
            jax.ShapeDtypeStruct((8, 128), F32),
        ),
        in_specs=[smem, vmem, any_spec, any_spec, any_spec],
        out_specs=(vmem, any_spec, any_spec, vmem),
        scratch_shapes=[
            vm(2, 4, entries, 8, 512), vm(2, 4, entries, 8, 512), vm(2, 2, 8, 4, 8, 512), vm(*piece),
            vm(*piece), vm(3, 2, 8, 4, 8, 512), vm(2, 4, cap, 8, 512), vm(2, 4, entries, 8, 512),
            vm(1, 32, 16, 512), vm(3, 512, 512), vm(3, 512, 512), vm(1, 128), vm(31, 1, 128), vm(4, 8, 128),
            vm(8, 128), vm(8, 128, dtype=jnp.int32), pltpu.SMEM((8, 128), jnp.int32),
            half(512, 512), half(512, 512), vm(512, 512), half(512, 512), half(512, 512), half(512, 512),
            half(512, 512), vm(512, 512), half(512, 512), half(512, 512), half(512, 512), half(512, 512),
            dma(4, 2, 3), dma(4, 2, 3), dma(6, 2, 7), dma(6, 2, 7), dma(10, 2), dma(31), dma(31), dma(3), dma(3),
            dma(4), dma(2, 3),
        ],
        name="step" + str(cap),
        compiler_params=pltpu.CompilerParams(collective_id=ident, has_side_effects=True, vmem_limit_bytes=58 * 2**20),
    )(assign, assign, gradient, left_stat, right_stat)


def body(gradient, left_stat, right_stat, assign):
    *outs, over = step(CAP, 0, assign, gradient, left_stat, right_stat)

    def again(_):
        return tuple(step(FULL, 1, assign, gradient, left_stat, right_stat)[:3])

    return lax.cond(over[1, 0] > 0.0, again, lambda kept: kept, tuple(outs))


def solution(mesh):
    placed = P("expert", None, "shard", None)
    slots = P("expert", "shard", None, None)
    return jax.shard_map(
        body,
        mesh=mesh,
        in_specs=(placed, slots, slots, P("expert", None)),
        out_specs=(placed, slots, slots),
        check_vma=False,
    )
```

```python
import functools

import jax
import jax.numpy as jnp
from jax import lax
from jax.experimental import pallas as pl
from jax.experimental.pallas import tpu as pltpu
from jax.sharding import PartitionSpec as P

MESH = pl.DeviceIdType.MESH
F32 = jnp.float32
BF16 = jnp.bfloat16
HALF = 256
CAP = 8
FULL = 16
LIST_A, LIST_B, OWNER, ENTRY_A, ENTRY_B, OVER = range(6)

C0 = 25.0 / 16.0
C1 = -5.0 / 16.0 - 3125.0 / 4096.0
C2 = 3125.0 / 4096.0
C3 = -1250.0 / 4096.0
C4 = 250.0 / 4096.0
C5 = -25.0 / 4096.0
C6 = 1.0 / 4096.0


def split(value):
    high = value.astype(BF16)
    return high, (value - high.astype(F32)).astype(BF16)


def dot(a, b, dims=((1,), (0,))):
    return lax.dot_general(a, b, (dims, ((), ())), preferred_element_type=F32)


def total(value):
    return jnp.sum(jnp.sum(value, axis=1, keepdims=True), axis=0, keepdims=True)


def part(i):
    return pl.ds(i * HALF, HALF)


def place(slot):
    d = (slot * 43) >> 7
    z, x, c = d >> 3, (d >> 1) & 3, d & 1
    return slot - 3 * d, z, x, d & 7, z * 2 + c


def fill_table(assign_ref, table_ref, row):
    shape = (128, 128)
    row[...] = jnp.full((8, 128), -1.0, F32)
    row[0:1, 0:96] = assign_ref[...].astype(F32)
    across = jnp.broadcast_to(row[0:1, :], shape)
    down = across.T
    i = lax.broadcasted_iota(jnp.int32, shape, 0)
    j = lax.broadcasted_iota(jnp.int32, shape, 1)
    rank_i, za_i, xa_i, _, _ = place(i)
    rank_j, za_j, xa_j, b0_j, b1_j = place(j)
    more_i = (down >= 0.0) & (rank_i > 0)
    more_j = (across >= 0.0) & (rank_j > 0)

    def count(mask, axis):
        return jnp.sum(jnp.where(mask, 1.0, 0.0), axis=axis, keepdims=True)

    over = jnp.zeros((1, 1), F32)
    for h, (ga_i, ga_j, b_j) in enumerate(((za_i, za_j, b0_j), (xa_i, xa_j, b1_j))):
        same = ga_i == ga_j
        before_i = count(more_j & same & (j < i), 1)
        before_j = count(more_i & same & (i < j), 0)
        listed = more_i & (ga_i == (j >> 4)) & (before_i == (j & 15).astype(F32))
        spots = jnp.sum(jnp.where(listed, i.astype(F32), 0.0), axis=0, keepdims=True)
        table_ref[LIST_A + h:LIST_A + h + 1, :] = jnp.minimum(spots, 95.0).astype(jnp.int32)
        entry = jnp.where(rank_j[0:1] == 0, b_j[0:1].astype(F32), 8.0 + before_j)
        table_ref[ENTRY_A + h:ENTRY_A + h + 1, :] = jnp.clip(entry, 0.0, 23.0).astype(jnp.int32)
        over = over + count(more_j[0:1] & (before_j >= float(CAP)), 1)
    owner = jnp.sum(jnp.where(down == j.astype(F32), i.astype(F32), 0.0), axis=0, keepdims=True)
    table_ref[OWNER:OWNER + 1, :] = jnp.minimum(owner, 95.0).astype(jnp.int32)
    table_ref[OVER:OVER + 1, :] = jnp.broadcast_to(over, (1, 128)).astype(jnp.int32)
    table_ref[OVER + 1:8, :] = jnp.zeros((7 - OVER, 128), jnp.int32)


def step_kernel(
    cap,
    assign_ref, row_ref, gradient_ref, left_ref, right_ref,
    update_ref, new_left_ref, new_right_ref, over_ref,
    sent, mid, pad, held, back, rmid, comp, fin,
    grad_ref, sums, sumv, sumy, row, table_v, table_ref,
    sh, sl, a_buf, xh, xl, yh, yl, base, plh, pll, prh, prl,
    a_s, a_r, b_s, b_r, loc, sum_s, sum_r, y_s, y_r, io_in,
):
    e = lax.axis_index("expert")
    me = lax.axis_index("shard")
    z, x, c = lax.div(me, 8), lax.rem(lax.div(me, 2), 4), lax.rem(me, 2)
    lbuf, rbuf = new_left_ref.at[0], new_right_ref.at[0]
    group = (z, x)
    spot = (x * 2 + c, z * 2 + c)

    def device(h, a, b):
        if h == 0:
            return (e, a * 8 + b)
        return (e, lax.div(b, 2) * 8 + a * 2 + lax.rem(b, 2))

    def index(h, a, b):
        return device(h, a, b)[1]

    barrier = pltpu.get_barrier_semaphore()
    for d in range(1, 4):
        pl.semaphore_signal(barrier, inc=1, device_id=(lax.rem(e + d, 4), me), device_id_type=MESH)
    for d in range(1, 32):
        pl.semaphore_signal(barrier, inc=1, device_id=(e, lax.rem(me + d, 32)), device_id_type=MESH)

    fetch = pltpu.make_async_copy(gradient_ref, grad_ref, io_in.at[2])
    fetch.start()
    def square_sum(b, acc):
        rows = grad_ref[0, b]
        sq = rows * rows
        for q in range(4):
            acc = acc + sq[0:8, q * 128:(q + 1) * 128] + sq[8:16, q * 128:(q + 1) * 128]
        return acc


    def look(line, at, top):
        return jnp.clip(table_ref[line, at], 0, top)

    def build_first(d, carry):
        block = jnp.clip(assign_ref[0, d * 3], 0, 31)
        rows = grad_ref[0, block]
        zd, xd, cd = lax.div(d, 8), lax.rem(lax.div(d, 2), 4), lax.rem(d, 2)
        sent[0, zd, xd * 2 + cd] = rows[0:8]
        sent[1, xd, zd * 2 + cd] = rows[8:16]
        return carry

    def build_more(n, carry):
        a, j = lax.div(n, cap), lax.rem(n, cap)
        for h in range(2):
            block = jnp.clip(assign_ref[0, look(LIST_A + h, a * 16 + j, 95)], 0, 31)
            sent[h, a, 8 + j] = grad_ref[0, block, h * 8:h * 8 + 8]
        return carry

    def build_pad(k):
        def one(b, carry):
            for h in range(2):
                entry = look(ENTRY_A + h, index(h, group[h], b) * 3 + k, 7 + cap)
                pad[k - 1, h, b] = mid[h, :, entry]
            return carry

        lax.fori_loop(0, 8, one, 0, unroll=4)

    def build_comp(j, carry):
        for h in range(2):
            rank, _, _, b0, b1 = place(look(LIST_A + h, group[h] * 16 + j, 95))
            comp[h, :, j] = rmid[rank, h, (b0, b1)[h]]
        return carry

    first, more = pl.ds(0, 8), pl.ds(8, cap)
    near, ring = (1, 3, 2), (1, 7, 2, 6, 3, 5, 4)

    def along(r, src, dst):
        out, here = [], []
        for d in near:
            for h in range(2):
                t = lax.rem(group[h] + d, 4)
                out.append(pltpu.make_async_remote_copy(
                    src_ref=src(h, t), dst_ref=dst(h, group[h]),
                    send_sem=a_s.at[r, h, d - 1], recv_sem=a_r.at[r, h, d - 1],
                    device_id=device(h, t, spot[h]), device_id_type=MESH))
        for h in range(2):
            here.append(pltpu.make_async_copy(src(h, group[h]), dst(h, group[h]), loc.at[r, h]))
        return out, here

    def within(r, src, dst):
        out, here = [], []
        for d in ring:
            for h in range(2):
                t = lax.rem(spot[h] + d, 8)
                out.append(pltpu.make_async_remote_copy(
                    src_ref=src(h, t), dst_ref=dst(h, spot[h]),
                    send_sem=b_s.at[r, h, d - 1], recv_sem=b_r.at[r, h, d - 1],
                    device_id=device(h, group[h], t), device_id_type=MESH))
        for h in range(2):
            here.append(pltpu.make_async_copy(src(h, spot[h]), dst(h, spot[h]), loc.at[4 + r, h]))
        return out, here

    def rows_of(ref, k):
        def pick(h, b):
            if h == 0:
                return ref.at[k, :, lax.div(b, 2), lax.rem(b, 2), 0]
            return ref.at[k, lax.div(b, 2), :, lax.rem(b, 2), 1]

        return pick

    out_first = lambda: along(0, lambda h, a: sent.at[h, a, first], lambda h, a: mid.at[h, a, first])
    out_more = lambda: along(1, lambda h, a: sent.at[h, a, more], lambda h, a: mid.at[h, a, more])
    to_first = lambda: within(0, lambda h, b: mid.at[h, :, b], rows_of(held, 0))
    to_more = lambda k: within(k, lambda h, b: pad.at[k - 1, h, b], rows_of(held, k))
    arrive = lambda k: within(k, lambda h, b: pad.at[0, h, b], rows_of(held, k))
    from_slot = lambda k: within(3 + k, rows_of(back, k), lambda h, b: rmid.at[k, h, b])
    in_first = lambda: along(2, lambda h, a: rmid.at[0, h, :, a], lambda h, a: fin.at[h, a, first])
    in_more = lambda: along(3, lambda h, a: comp.at[h, a], lambda h, a: fin.at[h, a, more])

    def start(copies):
        for copy in copies[0] + copies[1]:
            copy.start()

    def landed(copies):
        for copy in copies[0]:
            copy.wait_recv()
        for copy in copies[1]:
            copy.wait()

    def gone(copies):
        for copy in copies[0]:
            copy.wait_send()

    fetch.wait()
    lax.fori_loop(0, 32, build_first, 0, unroll=8)
    pl.semaphore_wait(barrier, 34)
    start(out_first())

    squares = lax.fori_loop(0, grad_ref.shape[1], square_sum, jnp.zeros((8, 128), F32), unroll=8)
    sums[...] = jnp.sum(squares, axis=0, keepdims=True)

    sum_copies = []
    for d in range(1, 32):
        sum_copies.append(pltpu.make_async_remote_copy(
            src_ref=sums, dst_ref=sumv.at[d - 1], send_sem=sum_s.at[d - 1], recv_sem=sum_r.at[d - 1],
            device_id=(e, lax.rem(me + d, 32)), device_id_type=MESH))
    for copy in sum_copies:
        copy.start()
    fill_table(row_ref, table_v, row)
    lists = pltpu.make_async_copy(table_v, table_ref, io_in.at[3])
    lists.start()
    lists.wait()
    lax.fori_loop(0, 4 * cap, build_more, 0, unroll=4)
    start(out_more())
    loads = [
        pltpu.make_async_copy(left_ref.at[0], lbuf, io_in.at[0]),
        pltpu.make_async_copy(right_ref.at[0], rbuf, io_in.at[1]),
    ]
    for copy in loads:
        copy.start()
    acc = sums[...]
    for d, copy in enumerate(sum_copies):
        copy.wait_recv()
        acc = acc + sumv[d]
    sumy[0, 0:1, :] = acc
    sumy[0, 1:2, :] = jnp.full((1, 128), table_ref[OVER, 0].astype(F32), F32)
    sumy[0, 2:8, :] = jnp.zeros((6, 128), F32)
    y_copies = []
    for d in range(1, 4):
        y_copies.append(pltpu.make_async_remote_copy(
            src_ref=sumy.at[0], dst_ref=sumy.at[d], send_sem=y_s.at[d - 1], recv_sem=y_r.at[d - 1],
            device_id=(lax.rem(e + d, 4), me), device_id_type=MESH))
    for copy in y_copies:
        copy.start()
    landed(out_first())
    start(to_first())
    acc = sumy[0]
    for d, copy in enumerate(y_copies):
        copy.wait_recv()
        acc = acc + sumy[d + 1]
    mean_square = total(acc[0:1, :]) / (4.0 * 32.0 * 512.0 * 512.0)
    factor = jnp.minimum(1.0, 1.0 / jnp.sqrt(mean_square + 1e-06))
    over_ref[...] = acc
    landed(out_more())
    build_pad(1)
    start(to_more(1))
    build_pad(2)
    start(to_more(2))
    for copy in loads:
        copy.wait()

    def put(high, low, i, j, value):
        a, b = split(value)
        high[part(i), part(j)] = a
        low[part(i), part(j)] = b

    def both(high, low, i, j, value):
        put(high, low, i, j, value)
        if i != j:
            put(high, low, j, i, value.T)

    tiles = ((0, 0), (0, 1), (1, 1))

    def root(square, oh, ol):
        norm = jnp.sqrt(square + 1e-06)
        inverse = 1.0 / norm
        for i in range(2):
            for j in range(2):
                put(xh, xl, i, j, a_buf[part(i), part(j)] * inverse)
        for i, j in tiles:
            low = dot(xh[part(i), :], xl[:, part(j)])
            other = low if i == j else dot(xh[part(j), :], xl[:, part(i)])
            value = dot(xh[part(i), :], xh[:, part(j)]) + (low + other.T)
            both(yh, yl, i, j, value)
            base[part(i), part(j)] = value
        for i, j in tiles:
            x3 = (
                dot(yh[part(i), :], xh[:, part(j)])
                + (dot(yh[part(i), :], xl[:, part(j)]) + dot(yl[part(i), :], xh[:, part(j)]))
            )
            x1 = a_buf[part(i), part(j)] * inverse
            x2 = base[part(i), part(j)]
            value = C1 * x1 + C2 * x2 + C3 * x3
            if i == j:
                rows = lax.broadcasted_iota(jnp.int32, (HALF, HALF), 0)
                cols = lax.broadcasted_iota(jnp.int32, (HALF, HALF), 1)
                value = value + jnp.where(rows == cols, C0, 0.0)
            base[part(i), part(j)] = value
            high = x3.astype(BF16)
            rest = (C4 * x1 + C5 * x2 + C6 * x3)
            oh[part(i), part(j)] = high
            ol[part(i), part(j)] = rest.astype(BF16)
            if i != j:
                oh[part(j), part(i)] = x3.T.astype(BF16)
                ol[part(j), part(i)] = rest.T.astype(BF16)
        for i, j in tiles:
            base[part(i), part(j)] += dot(oh[part(i), :], ol[:, part(j)])
        for i, j in tiles:
            both(oh, ol, i, j, base[part(i), part(j)])
        return jnp.sqrt(jnp.sqrt(norm))

    def stat(buf, k, live, high, low):
        square = jnp.zeros((1, 1), F32)

        def take(i, j, product):
            old = buf[k, part(i), part(j)]
            new = 0.95 * old + product
            a_buf[part(i), part(j)] = new
            buf[k, part(i), part(j)] = jnp.where(live, new, old)
            return total(new * new)

        for i, j in tiles:
            one = low(i, j)
            other = one if i == j else low(j, i)
            product = high(i, j) + (one + other.T)
            square = square + take(i, j, product)
            if i != j:
                square = square + take(j, i, product.T)
        return square

    def slot(k):
        live = assign_ref[0, me * 3 + k] >= 0
        graft = jnp.zeros((1, 1), F32)
        for i in range(2):
            for j in range(2):
                piece = held[k, 2 * i:2 * i + 2, :, :, :, :, part(j)].reshape(HALF, HALF) * factor
                graft = graft + total(piece * piece)
                put(sh, sl, i, j, piece)
        nt, tn = ((1,), (1,)), ((0,), (0,))
        left_scale = root(stat(
            lbuf, k, live,
            lambda i, j: dot(sh[part(i), :], sh[part(j), :], nt),
            lambda i, j: dot(sh[part(i), :], sl[part(j), :], nt)), plh, pll)
        right_scale = root(stat(
            rbuf, k, live,
            lambda i, j: dot(sh[:, part(i)], sh[:, part(j)], tn),
            lambda i, j: dot(sh[:, part(i)], sl[:, part(j)], tn)), prh, prl)

        for i in range(2):
            for j in range(2):
                put(xh, xl, i, j, dot(plh[part(i), :], sh[:, part(j)])
                    + (dot(plh[part(i), :], sl[:, part(j)]) + dot(pll[part(i), :], sh[:, part(j)])))
        square = jnp.zeros((1, 1), F32)
        scale = 1.0 / (left_scale * right_scale)
        for i in range(2):
            for j in range(2):
                value = dot(xh[part(i), :], prh[:, part(j)]) + (
                    dot(xh[part(i), :], prl[:, part(j)]) + dot(xl[part(i), :], prh[:, part(j)]))
                value = value * scale
                square = square + total(value * value)
                a_buf[part(i), part(j)] = value
        count = 512.0 * 512.0
        ratio = jnp.sqrt(graft / count + 1e-12) / jnp.sqrt(square / count + 1e-12)
        for i in range(2):
            back[k, 2 * i:2 * i + 2] = (a_buf[part(i), :] * ratio).reshape(2, 4, 2, 2, 8, 512)

    def turn(k, carry):
        landed(arrive(k))
        slot(k)
        start(from_slot(k))
        return carry

    lax.fori_loop(0, 3, turn, 0)
    landed(from_slot(0))
    start(in_first())
    landed(from_slot(1))
    landed(from_slot(2))
    lax.fori_loop(0, cap, build_comp, 0, unroll=4)
    start(in_more())
    gone(out_first())
    gone(out_more())
    gone(to_first())
    gone(to_more(1))
    gone(to_more(2))
    for k in range(3):
        gone(from_slot(k))
    for copy in sum_copies + y_copies:
        copy.wait_send()
    for copies in (in_first(), in_more()):
        landed(copies)
        gone(copies)

    def take(b, carry):
        s = look(OWNER, b, 95)
        _, za, xa, _, _ = place(s)
        for h, a in enumerate((za, xa)):
            entry = look(ENTRY_A + h, s, 7 + cap)
            update_ref[0, b, h * 8:h * 8 + 8] = fin[h, a, entry]
        return carry

    lax.fori_loop(0, update_ref.shape[1], take, 0, unroll=4)


def step(cap, ident, assign, gradient, left_stat, right_stat):
    vm = lambda *shape, dtype=F32: pltpu.VMEM(shape, dtype)
    half = lambda *shape: pltpu.VMEM(shape, BF16)
    dma = lambda *shape: pltpu.SemaphoreType.DMA(shape)
    any_spec = pl.BlockSpec(memory_space=pl.ANY)
    smem = pl.BlockSpec(memory_space=pltpu.SMEM)
    vmem = pl.BlockSpec(memory_space=pltpu.VMEM)
    entries = 8 + cap
    piece = (3, 4, 4, 2, 2, 8, 512)
    return pl.pallas_call(
        functools.partial(step_kernel, cap),
        out_shape=(
            jax.ShapeDtypeStruct(gradient.shape, F32),
            jax.ShapeDtypeStruct(left_stat.shape, F32),
            jax.ShapeDtypeStruct(right_stat.shape, F32),
            jax.ShapeDtypeStruct((8, 128), F32),
        ),
        in_specs=[smem, vmem, any_spec, any_spec, any_spec],
        out_specs=(vmem, vmem, vmem, vmem),
        scratch_shapes=[
            vm(2, 4, entries, 8, 512), vm(2, 4, entries, 8, 512), vm(2, 2, 8, 4, 8, 512), vm(*piece),
            vm(*piece), vm(3, 2, 8, 4, 8, 512), vm(2, 4, cap, 8, 512), vm(2, 4, entries, 8, 512),
            vm(1, 32, 16, 512), vm(1, 128), vm(31, 1, 128), vm(4, 8, 128),
            vm(8, 128), vm(8, 128, dtype=jnp.int32), pltpu.SMEM((8, 128), jnp.int32),
            half(512, 512), half(512, 512), vm(512, 512), half(512, 512), half(512, 512), half(512, 512),
            half(512, 512), vm(512, 512), half(512, 512), half(512, 512), half(512, 512), half(512, 512),
            dma(4, 2, 3), dma(4, 2, 3), dma(6, 2, 7), dma(6, 2, 7), dma(10, 2), dma(31), dma(31), dma(3), dma(3),
            dma(4),
        ],
        name="step" + str(cap),
        compiler_params=pltpu.CompilerParams(collective_id=ident, has_side_effects=True, vmem_limit_bytes=(44 if cap == CAP else 63) * 2**20),
    )(assign, assign, gradient, left_stat, right_stat)


def store_kernel(update_in, left_in, right_in, update_out, left_out, right_out):
    left_out[...] = left_in[...]
    right_out[...] = right_in[...]

    @pl.when(pl.program_id(0) == 0)
    def _():
        update_out[...] = update_in[...]


def store(outs):
    slot_spec = pl.BlockSpec((1, 1, 512, 512), lambda k: (0, k, 0, 0))
    whole = pl.BlockSpec((1, 32, 16, 512), lambda k: (0, 0, 0, 0))
    return pl.pallas_call(
        store_kernel,
        grid=(3,),
        out_shape=tuple(jax.ShapeDtypeStruct(out.shape, out.dtype) for out in outs),
        in_specs=[whole, slot_spec, slot_spec],
        out_specs=(whole, slot_spec, slot_spec),
        name="store",
        compiler_params=pltpu.CompilerParams(vmem_limit_bytes=30 * 2**20),
    )(*outs)


def body(gradient, left_stat, right_stat, assign):
    *outs, over = step(CAP, 0, assign, gradient, left_stat, right_stat)

    def again(_):
        return store(step(FULL, 1, assign, gradient, left_stat, right_stat)[:3])

    return lax.cond(over[1, 0] > 0.0, again, lambda kept: kept, store(outs))


def solution(mesh):
    placed = P("expert", None, "shard", None)
    slots = P("expert", "shard", None, None)
    return jax.shard_map(
        body,
        mesh=mesh,
        in_specs=(placed, slots, slots, P("expert", None)),
        out_specs=(placed, slots, slots),
        check_vma=False,
    )
```

```python
import functools

import jax
import jax.numpy as jnp
from jax import lax
from jax.experimental import pallas as pl
from jax.experimental.pallas import tpu as pltpu
from jax.sharding import PartitionSpec as P

MESH = pl.DeviceIdType.MESH
F32 = jnp.float32
BF16 = jnp.bfloat16
HALF = 256
CAP = 8
FULL = 16
LIST_A, LIST_B, OWNER, ENTRY_A, ENTRY_B, OVER = range(6)

C0 = 25.0 / 16.0
C1 = -5.0 / 16.0 - 3125.0 / 4096.0
C2 = 3125.0 / 4096.0
C3 = -1250.0 / 4096.0
C4 = 250.0 / 4096.0
C5 = -25.0 / 4096.0
C6 = 1.0 / 4096.0


def split(value):
    high = value.astype(BF16)
    return high, (value - high.astype(F32)).astype(BF16)


def dot(a, b, dims=((1,), (0,))):
    return lax.dot_general(a, b, (dims, ((), ())), preferred_element_type=F32)


def total(value):
    return jnp.sum(jnp.sum(value, axis=1, keepdims=True), axis=0, keepdims=True)


def part(i):
    return pl.ds(i * HALF, HALF)


def place(slot):
    d = (slot * 43) >> 7
    z, x, c = d >> 3, (d >> 1) & 3, d & 1
    return slot - 3 * d, z, x, d & 7, z * 2 + c


def fill_table(assign_ref, table_ref, row):
    shape = (128, 128)
    row[...] = jnp.full((8, 128), -1.0, F32)
    row[0:1, 0:96] = assign_ref[...].astype(F32)
    across = jnp.broadcast_to(row[0:1, :], shape)
    down = across.T
    i = lax.broadcasted_iota(jnp.int32, shape, 0)
    j = lax.broadcasted_iota(jnp.int32, shape, 1)
    rank_i, za_i, xa_i, _, _ = place(i)
    rank_j, za_j, xa_j, b0_j, b1_j = place(j)
    more_i = (down >= 0.0) & (rank_i > 0)
    more_j = (across >= 0.0) & (rank_j > 0)

    def count(mask, axis):
        return jnp.sum(jnp.where(mask, 1.0, 0.0), axis=axis, keepdims=True)

    over = jnp.zeros((1, 1), F32)
    for h, (ga_i, ga_j, b_j) in enumerate(((za_i, za_j, b0_j), (xa_i, xa_j, b1_j))):
        same = ga_i == ga_j
        before_i = count(more_j & same & (j < i), 1)
        before_j = count(more_i & same & (i < j), 0)
        listed = more_i & (ga_i == (j >> 4)) & (before_i == (j & 15).astype(F32))
        spots = jnp.sum(jnp.where(listed, i.astype(F32), 0.0), axis=0, keepdims=True)
        table_ref[LIST_A + h:LIST_A + h + 1, :] = jnp.minimum(spots, 95.0).astype(jnp.int32)
        entry = jnp.where(rank_j[0:1] == 0, b_j[0:1].astype(F32), 8.0 + before_j)
        table_ref[ENTRY_A + h:ENTRY_A + h + 1, :] = jnp.clip(entry, 0.0, 23.0).astype(jnp.int32)
        over = over + count(more_j[0:1] & (before_j >= float(CAP)), 1)
    owner = jnp.sum(jnp.where(down == j.astype(F32), i.astype(F32), 0.0), axis=0, keepdims=True)
    table_ref[OWNER:OWNER + 1, :] = jnp.minimum(owner, 95.0).astype(jnp.int32)
    table_ref[OVER:OVER + 1, :] = jnp.broadcast_to(over, (1, 128)).astype(jnp.int32)
    table_ref[OVER + 1:8, :] = jnp.zeros((7 - OVER, 128), jnp.int32)


def step_kernel(
    cap,
    slots_ref, gradient_ref, left_ref, right_ref,
    update_ref, new_left_ref, new_right_ref, over_ref,
    sent, mid, pad, held, back, rmid, comp, fin,
    assign_ref, row_ref, grad_ref, sums, sumv, row, table_v, table_ref,
    sh, sl, a_buf, xh, xl, yh, yl, base, plh, pll, prh, prl,
    a_s, a_r, b_s, b_r, loc, sum_s, sum_r, io_in,
):
    e = lax.axis_index("expert")
    me = lax.axis_index("shard")
    z, x, c = lax.div(me, 8), lax.rem(lax.div(me, 2), 4), lax.rem(me, 2)
    lbuf, rbuf = new_left_ref.at[0], new_right_ref.at[0]
    group = (z, x)
    spot = (x * 2 + c, z * 2 + c)

    def device(h, a, b):
        if h == 0:
            return (e, a * 8 + b)
        return (e, lax.div(b, 2) * 8 + a * 2 + lax.rem(b, 2))

    def index(h, a, b):
        return device(h, a, b)[1]

    fetches = [
        pltpu.make_async_copy(slots_ref, assign_ref, io_in.at[4]),
        pltpu.make_async_copy(gradient_ref, grad_ref, io_in.at[2]),
        pltpu.make_async_copy(slots_ref, row_ref, io_in.at[5]),
    ]
    for copy in fetches:
        copy.start()
    barrier = pltpu.get_barrier_semaphore()
    for d in range(1, 8):
        pl.semaphore_signal(barrier, inc=1, device_id=device(0, z, lax.rem(spot[0] + d, 8)), device_id_type=MESH)
    for d in range(1, 4):
        for f in range(2):
            pl.semaphore_signal(
                barrier, inc=1, device_id=(e, lax.rem(z + d, 4) * 8 + x * 2 + lax.rem(c + f, 2)), device_id_type=MESH)
    for d in range(1, 4):
        pl.semaphore_signal(barrier, inc=1, device_id=(lax.rem(e + d, 4), me), device_id_type=MESH)

    def square_sum(b, acc):
        rows = grad_ref[0, b]
        sq = rows * rows
        for q in range(4):
            acc = acc + sq[0:8, q * 128:(q + 1) * 128] + sq[8:16, q * 128:(q + 1) * 128]
        return acc


    def look(line, at, top):
        return jnp.clip(table_ref[line, at], 0, top)

    def build_first(d, carry):
        block = jnp.clip(assign_ref[0, d * 3], 0, 31)
        rows = grad_ref[0, block]
        zd, xd, cd = lax.div(d, 8), lax.rem(lax.div(d, 2), 4), lax.rem(d, 2)
        sent[0, zd, xd * 2 + cd] = rows[0:8]
        sent[1, xd, zd * 2 + cd] = rows[8:16]
        return carry

    def build_more(n, carry):
        a, j = lax.div(n, cap), lax.rem(n, cap)
        for h in range(2):
            block = jnp.clip(assign_ref[0, look(LIST_A + h, a * 16 + j, 95)], 0, 31)
            sent[h, a, 8 + j] = grad_ref[0, block, h * 8:h * 8 + 8]
        return carry

    def build_pad(k):
        def one(b, carry):
            for h in range(2):
                entry = look(ENTRY_A + h, index(h, group[h], b) * 3 + k, 7 + cap)
                pad[k - 1, h, b] = mid[h, :, entry]
            return carry

        lax.fori_loop(0, 8, one, 0, unroll=4)

    def build_comp(j, carry):
        for h in range(2):
            rank, _, _, b0, b1 = place(look(LIST_A + h, group[h] * 16 + j, 95))
            comp[h, :, j] = rmid[rank, h, (b0, b1)[h]]
        return carry

    first, more = pl.ds(0, 8), pl.ds(8, cap)
    near, ring = (1, 3, 2), (1, 7, 2, 6, 3, 5, 4)

    def along(r, src, dst):
        out, here = [], []
        for d in near:
            for h in range(2):
                t = lax.rem(group[h] + d, 4)
                out.append(pltpu.make_async_remote_copy(
                    src_ref=src(h, t), dst_ref=dst(h, group[h]),
                    send_sem=a_s.at[r, h, d - 1], recv_sem=a_r.at[r, h, d - 1],
                    device_id=device(h, t, spot[h]), device_id_type=MESH))
        for h in range(2):
            here.append(pltpu.make_async_copy(src(h, group[h]), dst(h, group[h]), loc.at[r, h]))
        return out, here

    def within(r, src, dst):
        out, here = [], []
        for d in ring:
            for h in range(2):
                t = lax.rem(spot[h] + d, 8)
                out.append(pltpu.make_async_remote_copy(
                    src_ref=src(h, t), dst_ref=dst(h, spot[h]),
                    send_sem=b_s.at[r, h, d - 1], recv_sem=b_r.at[r, h, d - 1],
                    device_id=device(h, group[h], t), device_id_type=MESH))
        for h in range(2):
            here.append(pltpu.make_async_copy(src(h, spot[h]), dst(h, spot[h]), loc.at[4 + r, h]))
        return out, here

    def rows_of(ref, k):
        def pick(h, b):
            if h == 0:
                return ref.at[k, :, lax.div(b, 2), lax.rem(b, 2), 0]
            return ref.at[k, lax.div(b, 2), :, lax.rem(b, 2), 1]

        return pick

    out_first = lambda: along(0, lambda h, a: sent.at[h, a, first], lambda h, a: mid.at[h, a, first])
    out_more = lambda: along(1, lambda h, a: sent.at[h, a, more], lambda h, a: mid.at[h, a, more])
    to_first = lambda: within(0, lambda h, b: mid.at[h, :, b], rows_of(held, 0))
    to_more = lambda k: within(k, lambda h, b: pad.at[k - 1, h, b], rows_of(held, k))
    arrive = lambda k: within(k, lambda h, b: pad.at[0, h, b], rows_of(held, k))
    from_slot = lambda k: within(3 + k, rows_of(back, k), lambda h, b: rmid.at[k, h, b])
    in_first = lambda: along(2, lambda h, a: rmid.at[0, h, :, a], lambda h, a: fin.at[h, a, first])
    in_more = lambda: along(3, lambda h, a: comp.at[h, a], lambda h, a: fin.at[h, a, more])

    def start(copies):
        for copy in copies[0] + copies[1]:
            copy.start()

    def landed(copies):
        for copy in copies[0]:
            copy.wait_recv()
        for copy in copies[1]:
            copy.wait()

    def gone(copies):
        for copy in copies[0]:
            copy.wait_send()

    for copy in fetches:
        copy.wait()
    lax.fori_loop(0, 32, build_first, 0, unroll=8)
    pl.semaphore_wait(barrier, 16)
    start(out_first())

    fill_table(row_ref, table_v, row)
    lists = pltpu.make_async_copy(table_v, table_ref, io_in.at[3])
    lists.start()
    squares = lax.fori_loop(0, grad_ref.shape[1], square_sum, jnp.zeros((8, 128), F32), unroll=8)
    sums[0, 0:1, :] = jnp.sum(squares, axis=0, keepdims=True)
    sums[0, 1:2, :] = table_v[OVER:OVER + 1, :].astype(F32)
    sums[0, 2:8, :] = jnp.zeros((6, 128), F32)
    sum_copies = []

    def sum_send(stage, at, peers):
        copies = []
        for i, peer in enumerate(peers):
            copies.append(pltpu.make_async_remote_copy(
                src_ref=sums.at[stage], dst_ref=sumv.at[at + i],
                send_sem=sum_s.at[at + i], recv_sem=sum_r.at[at + i],
                device_id=peer, device_id_type=MESH))
        for copy in copies:
            copy.start()
        sum_copies.extend(copies)
        return copies

    def sum_take(stage, at, copies):
        acc = sums[stage]
        for i, copy in enumerate(copies):
            copy.wait_recv()
            acc = acc + sumv[at + i]
        sums[stage + 1] = acc

    s0 = sum_send(0, 0, [(lax.rem(e + d, 4), me) for d in range(1, 4)])
    lists.wait()
    lax.fori_loop(0, 4 * cap, build_more, 0, unroll=4)
    sum_take(0, 0, s0)
    s1 = sum_send(1, 3, [device(0, lax.rem(z + d, 4), spot[0]) for d in range(1, 4)])
    start(out_more())
    loads = [
        pltpu.make_async_copy(left_ref.at[0], lbuf, io_in.at[0]),
        pltpu.make_async_copy(right_ref.at[0], rbuf, io_in.at[1]),
    ]
    for copy in loads:
        copy.start()
    landed(out_first())
    sum_take(1, 3, s1)
    s2 = sum_send(2, 6, [device(0, z, lax.rem(spot[0] + d, 8)) for d in range(1, 8)])
    start(to_first())
    landed(out_more())
    build_pad(1)
    start(to_more(1))
    build_pad(2)
    start(to_more(2))
    sum_take(2, 6, s2)
    mean_square = total(sums[3, 0:1, :]) / (4.0 * 32.0 * 512.0 * 512.0)
    factor = jnp.minimum(1.0, 1.0 / jnp.sqrt(mean_square + 1e-06))
    over_ref[...] = sums[3]
    for copy in loads:
        copy.wait()

    def put(high, low, i, j, value):
        a, b = split(value)
        high[part(i), part(j)] = a
        low[part(i), part(j)] = b

    def both(high, low, i, j, value):
        put(high, low, i, j, value)
        if i != j:
            put(high, low, j, i, value.T)

    tiles = ((0, 0), (0, 1), (1, 1))

    def root(square, oh, ol):
        norm = jnp.sqrt(square + 1e-06)
        inverse = 1.0 / norm
        for i in range(2):
            for j in range(2):
                put(xh, xl, i, j, a_buf[part(i), part(j)] * inverse)
        for i, j in tiles:
            low = dot(xh[part(i), :], xl[:, part(j)])
            other = low if i == j else dot(xh[part(j), :], xl[:, part(i)])
            value = dot(xh[part(i), :], xh[:, part(j)]) + (low + other.T)
            both(yh, yl, i, j, value)
            base[part(i), part(j)] = value
        for i, j in tiles:
            x3 = (
                dot(yh[part(i), :], xh[:, part(j)])
                + (dot(yh[part(i), :], xl[:, part(j)]) + dot(yl[part(i), :], xh[:, part(j)]))
            )
            x1 = a_buf[part(i), part(j)] * inverse
            x2 = base[part(i), part(j)]
            value = C1 * x1 + C2 * x2 + C3 * x3
            if i == j:
                rows = lax.broadcasted_iota(jnp.int32, (HALF, HALF), 0)
                cols = lax.broadcasted_iota(jnp.int32, (HALF, HALF), 1)
                value = value + jnp.where(rows == cols, C0, 0.0)
            base[part(i), part(j)] = value
            high = x3.astype(BF16)
            rest = (C4 * x1 + C5 * x2 + C6 * x3)
            oh[part(i), part(j)] = high
            ol[part(i), part(j)] = rest.astype(BF16)
            if i != j:
                oh[part(j), part(i)] = x3.T.astype(BF16)
                ol[part(j), part(i)] = rest.T.astype(BF16)
        for i, j in tiles:
            base[part(i), part(j)] += dot(oh[part(i), :], ol[:, part(j)])
        for i, j in tiles:
            both(oh, ol, i, j, base[part(i), part(j)])
        return jnp.sqrt(jnp.sqrt(norm))

    def stat(buf, k, live, high, low):
        square = jnp.zeros((1, 1), F32)

        def take(i, j, product):
            old = buf[k, part(i), part(j)]
            new = 0.95 * old + product
            a_buf[part(i), part(j)] = new
            buf[k, part(i), part(j)] = jnp.where(live, new, old)
            return total(new * new)

        for i, j in tiles:
            one = low(i, j)
            other = one if i == j else low(j, i)
            product = high(i, j) + (one + other.T)
            square = square + take(i, j, product)
            if i != j:
                square = square + take(j, i, product.T)
        return square

    def slot(k):
        live = assign_ref[0, me * 3 + k] >= 0
        graft = jnp.zeros((1, 1), F32)
        for i in range(2):
            for j in range(2):
                piece = held[k, 2 * i:2 * i + 2, :, :, :, :, part(j)].reshape(HALF, HALF) * factor
                graft = graft + total(piece * piece)
                put(sh, sl, i, j, piece)
        nt, tn = ((1,), (1,)), ((0,), (0,))
        left_scale = root(stat(
            lbuf, k, live,
            lambda i, j: dot(sh[part(i), :], sh[part(j), :], nt),
            lambda i, j: dot(sh[part(i), :], sl[part(j), :], nt)), plh, pll)
        right_scale = root(stat(
            rbuf, k, live,
            lambda i, j: dot(sh[:, part(i)], sh[:, part(j)], tn),
            lambda i, j: dot(sh[:, part(i)], sl[:, part(j)], tn)), prh, prl)

        for i in range(2):
            for j in range(2):
                put(xh, xl, i, j, dot(plh[part(i), :], sh[:, part(j)])
                    + (dot(plh[part(i), :], sl[:, part(j)]) + dot(pll[part(i), :], sh[:, part(j)])))
        square = jnp.zeros((1, 1), F32)
        scale = 1.0 / (left_scale * right_scale)
        for i in range(2):
            for j in range(2):
                value = dot(xh[part(i), :], prh[:, part(j)]) + (
                    dot(xh[part(i), :], prl[:, part(j)]) + dot(xl[part(i), :], prh[:, part(j)]))
                value = value * scale
                square = square + total(value * value)
                a_buf[part(i), part(j)] = value
        count = 512.0 * 512.0
        ratio = jnp.sqrt(graft / count + 1e-12) / jnp.sqrt(square / count + 1e-12)
        for i in range(2):
            back[k, 2 * i:2 * i + 2] = (a_buf[part(i), :] * ratio).reshape(2, 4, 2, 2, 8, 512)

    def turn(k, carry):
        landed(arrive(k))
        slot(k)
        start(from_slot(k))
        return carry

    lax.fori_loop(0, 3, turn, 0)
    landed(from_slot(0))
    start(in_first())
    landed(from_slot(1))
    landed(from_slot(2))
    lax.fori_loop(0, cap, build_comp, 0, unroll=4)
    start(in_more())
    gone(out_first())
    gone(out_more())
    gone(to_first())
    gone(to_more(1))
    gone(to_more(2))
    for k in range(3):
        gone(from_slot(k))
    for copy in sum_copies:
        copy.wait_send()
    for copies in (in_first(), in_more()):
        landed(copies)
        gone(copies)

    def take(b, carry):
        s = look(OWNER, b, 95)
        _, za, xa, _, _ = place(s)
        for h, a in enumerate((za, xa)):
            entry = look(ENTRY_A + h, s, 7 + cap)
            update_ref[0, b, h * 8:h * 8 + 8] = fin[h, a, entry]
        return carry

    lax.fori_loop(0, update_ref.shape[1], take, 0, unroll=4)


def step(cap, ident, assign, gradient, left_stat, right_stat):
    vm = lambda *shape, dtype=F32: pltpu.VMEM(shape, dtype)
    half = lambda *shape: pltpu.VMEM(shape, BF16)
    dma = lambda *shape: pltpu.SemaphoreType.DMA(shape)
    any_spec = pl.BlockSpec(memory_space=pl.ANY)
    vmem = pl.BlockSpec(memory_space=pltpu.VMEM)
    entries = 8 + cap
    piece = (3, 4, 4, 2, 2, 8, 512)
    return pl.pallas_call(
        functools.partial(step_kernel, cap),
        out_shape=(
            jax.ShapeDtypeStruct(gradient.shape, F32),
            jax.ShapeDtypeStruct(left_stat.shape, F32),
            jax.ShapeDtypeStruct(right_stat.shape, F32),
            jax.ShapeDtypeStruct((8, 128), F32),
        ),
        in_specs=[any_spec] * 4,
        out_specs=(vmem, vmem, vmem, vmem),
        scratch_shapes=[
            vm(2, 4, entries, 8, 512), vm(2, 4, entries, 8, 512), vm(2, 2, 8, 4, 8, 512), vm(*piece),
            vm(*piece), vm(3, 2, 8, 4, 8, 512), vm(2, 4, cap, 8, 512), vm(2, 4, entries, 8, 512),
            pltpu.SMEM((1, 96), jnp.int32), vm(1, 96, dtype=jnp.int32), vm(1, 32, 16, 512), vm(4, 8, 128), vm(13, 8, 128),
            vm(8, 128), vm(8, 128, dtype=jnp.int32), pltpu.SMEM((8, 128), jnp.int32),
            half(512, 512), half(512, 512), vm(512, 512), half(512, 512), half(512, 512), half(512, 512),
            half(512, 512), vm(512, 512), half(512, 512), half(512, 512), half(512, 512), half(512, 512),
            dma(4, 2, 3), dma(4, 2, 3), dma(6, 2, 7), dma(6, 2, 7), dma(10, 2), dma(13), dma(13),
            dma(6),
        ],
        name="step" + str(cap),
        compiler_params=pltpu.CompilerParams(collective_id=ident, has_side_effects=True, vmem_limit_bytes=(44 if cap == CAP else 63) * 2**20),
    )(assign, gradient, left_stat, right_stat)


def store_kernel(update_in, left_in, right_in, update_out, left_out, right_out):
    left_out[...] = left_in[...]
    right_out[...] = right_in[...]

    @pl.when(pl.program_id(0) == 0)
    def _():
        update_out[...] = update_in[...]


def store(outs):
    slot_spec = pl.BlockSpec((1, 1, 512, 512), lambda k: (0, k, 0, 0))
    whole = pl.BlockSpec((1, 32, 16, 512), lambda k: (0, 0, 0, 0))
    return pl.pallas_call(
        store_kernel,
        grid=(3,),
        out_shape=tuple(jax.ShapeDtypeStruct(out.shape, out.dtype) for out in outs),
        in_specs=[whole, slot_spec, slot_spec],
        out_specs=(whole, slot_spec, slot_spec),
        name="store",
        compiler_params=pltpu.CompilerParams(vmem_limit_bytes=30 * 2**20),
    )(*outs)


def body(gradient, left_stat, right_stat, assign):
    *outs, over = step(CAP, 0, assign, gradient, left_stat, right_stat)

    def again(_):
        return store(step(FULL, 1, assign, gradient, left_stat, right_stat)[:3])

    return lax.cond(over[1, 0] > 0.0, again, lambda kept: kept, store(outs))


def solution(mesh):
    placed = P("expert", None, "shard", None)
    slots = P("expert", "shard", None, None)
    return jax.shard_map(
        body,
        mesh=mesh,
        in_specs=(placed, slots, slots, P("expert", None)),
        out_specs=(placed, slots, slots),
        check_vma=False,
    )
```

```python
import functools

import jax
import jax.numpy as jnp
from jax import lax
from jax.experimental import pallas as pl
from jax.experimental.pallas import tpu as pltpu
from jax.sharding import PartitionSpec as P

MESH = pl.DeviceIdType.MESH
F32 = jnp.float32
BF16 = jnp.bfloat16
HALF = 256
CAP = 8
FULL = 16
LIST_A, LIST_B, OWNER, ENTRY_A, ENTRY_B, OVER = range(6)

C0 = 25.0 / 16.0
C1 = -5.0 / 16.0 - 3125.0 / 4096.0
C2 = 3125.0 / 4096.0
C3 = -1250.0 / 4096.0
C4 = 250.0 / 4096.0
C5 = -25.0 / 4096.0
C6 = 1.0 / 4096.0


def split(value):
    high = value.astype(BF16)
    return high, (value - high.astype(F32)).astype(BF16)


def dot(a, b, dims=((1,), (0,))):
    return lax.dot_general(a, b, (dims, ((), ())), preferred_element_type=F32)


def total(value):
    return jnp.sum(jnp.sum(value, axis=1, keepdims=True), axis=0, keepdims=True)


def part(i):
    return pl.ds(i * HALF, HALF)


def place(slot):
    d = (slot * 43) >> 7
    z, x, c = d >> 3, (d >> 1) & 3, d & 1
    return slot - 3 * d, z, x, d & 7, z * 2 + c


def fill_table(assign_ref, table_ref, row):
    shape = (128, 128)
    row[...] = jnp.full((8, 128), -1.0, F32)
    row[0:1, 0:96] = assign_ref[...].astype(F32)
    across = jnp.broadcast_to(row[0:1, :], shape)
    down = across.T
    i = lax.broadcasted_iota(jnp.int32, shape, 0)
    j = lax.broadcasted_iota(jnp.int32, shape, 1)
    rank_i, za_i, xa_i, _, _ = place(i)
    rank_j, za_j, xa_j, b0_j, b1_j = place(j)
    more_i = (down >= 0.0) & (rank_i > 0)
    more_j = (across >= 0.0) & (rank_j > 0)

    def count(mask, axis):
        return jnp.sum(jnp.where(mask, 1.0, 0.0), axis=axis, keepdims=True)

    over = jnp.zeros((1, 1), F32)
    for h, (ga_i, ga_j, b_j) in enumerate(((za_i, za_j, b0_j), (xa_i, xa_j, b1_j))):
        same = ga_i == ga_j
        before_i = count(more_j & same & (j < i), 1)
        before_j = count(more_i & same & (i < j), 0)
        listed = more_i & (ga_i == (j >> 4)) & (before_i == (j & 15).astype(F32))
        spots = jnp.sum(jnp.where(listed, i.astype(F32), 0.0), axis=0, keepdims=True)
        table_ref[LIST_A + h:LIST_A + h + 1, :] = jnp.minimum(spots, 95.0).astype(jnp.int32)
        entry = jnp.where(rank_j[0:1] == 0, b_j[0:1].astype(F32), 8.0 + before_j)
        table_ref[ENTRY_A + h:ENTRY_A + h + 1, :] = jnp.clip(entry, 0.0, 23.0).astype(jnp.int32)
        over = over + count(more_j[0:1] & (before_j >= float(CAP)), 1)
    owner = jnp.sum(jnp.where(down == j.astype(F32), i.astype(F32), 0.0), axis=0, keepdims=True)
    table_ref[OWNER:OWNER + 1, :] = jnp.minimum(owner, 95.0).astype(jnp.int32)
    table_ref[OVER:OVER + 1, :] = jnp.broadcast_to(over, (1, 128)).astype(jnp.int32)
    table_ref[OVER + 1:8, :] = jnp.zeros((7 - OVER, 128), jnp.int32)


def step_kernel(
    cap,
    slots_ref, gradient_ref, left_ref, right_ref,
    update_ref, new_left_ref, new_right_ref, over_ref,
    sent, mid, pad, held, back, rmid, comp, fin,
    assign_ref, row_ref, grad_ref, sums, sumv, flags, row, table_v, table_ref,
    sh, sl, a_buf, base, xh, xl, yh, oh, ol,
    a_s, a_r, b_s, b_r, loc, sum_s, sum_r, flag_s, flag_r, io_in,
):
    e = lax.axis_index("expert")
    me = lax.axis_index("shard")
    z, x, c = lax.div(me, 8), lax.rem(lax.div(me, 2), 4), lax.rem(me, 2)
    lbuf, rbuf = new_left_ref.at[0], new_right_ref.at[0]
    group = (z, x)
    spot = (x * 2 + c, z * 2 + c)

    def device(h, a, b):
        if h == 0:
            return (e, a * 8 + b)
        return (e, lax.div(b, 2) * 8 + a * 2 + lax.rem(b, 2))

    def index(h, a, b):
        return device(h, a, b)[1]

    fetches = [
        pltpu.make_async_copy(slots_ref, assign_ref, io_in.at[4]),
        pltpu.make_async_copy(gradient_ref, grad_ref, io_in.at[2]),
        pltpu.make_async_copy(slots_ref, row_ref, io_in.at[5]),
    ]
    for copy in fetches:
        copy.start()
    barrier = pltpu.get_barrier_semaphore()
    for d in range(1, 8):
        pl.semaphore_signal(barrier, inc=1, device_id=device(0, z, lax.rem(spot[0] + d, 8)), device_id_type=MESH)
    for d in range(1, 4):
        for f in range(2):
            pl.semaphore_signal(
                barrier, inc=1, device_id=(e, lax.rem(z + d, 4) * 8 + x * 2 + lax.rem(c + f, 2)), device_id_type=MESH)
    for d in range(1, 4):
        pl.semaphore_signal(barrier, inc=1, device_id=(lax.rem(e + d, 4), me), device_id_type=MESH)

    def square_sum(b, acc):
        rows = grad_ref[0, b]
        sq = rows * rows
        for q in range(4):
            acc = acc + sq[0:8, q * 128:(q + 1) * 128] + sq[8:16, q * 128:(q + 1) * 128]
        return acc


    def look(line, at, top):
        return jnp.clip(table_ref[line, at], 0, top)

    def build_first(d, carry):
        block = jnp.clip(assign_ref[0, d * 3], 0, 31)
        rows = grad_ref[0, block]
        zd, xd, cd = lax.div(d, 8), lax.rem(lax.div(d, 2), 4), lax.rem(d, 2)
        sent[0, zd, xd * 2 + cd] = rows[0:8]
        sent[1, xd, zd * 2 + cd] = rows[8:16]
        return carry

    def build_more(n, carry):
        a, j = lax.div(n, cap), lax.rem(n, cap)
        for h in range(2):
            block = jnp.clip(assign_ref[0, look(LIST_A + h, a * 16 + j, 95)], 0, 31)
            sent[h, a, 8 + j] = grad_ref[0, block, h * 8:h * 8 + 8]
        return carry

    def build_pad(k):
        def one(b, carry):
            for h in range(2):
                entry = look(ENTRY_A + h, index(h, group[h], b) * 3 + k, 7 + cap)
                pad[k - 1, h, b] = mid[h, :, entry]
            return carry

        lax.fori_loop(0, 8, one, 0, unroll=4)

    def build_comp(j, carry):
        for h in range(2):
            rank, _, _, b0, b1 = place(look(LIST_A + h, group[h] * 16 + j, 95))
            comp[h, :, j] = rmid[rank, h, (b0, b1)[h]]
        return carry

    first, more = pl.ds(0, 8), pl.ds(8, cap)
    near, ring = (2, 1, 3), (4, 3, 5, 2, 6, 1, 7)

    def along(r, src, dst):
        out, here = [], []
        for d in near:
            for h in range(2):
                t = lax.rem(group[h] + d, 4)
                out.append(pltpu.make_async_remote_copy(
                    src_ref=src(h, t), dst_ref=dst(h, group[h]),
                    send_sem=a_s.at[r, h, d - 1], recv_sem=a_r.at[r, h, d - 1],
                    device_id=device(h, t, spot[h]), device_id_type=MESH))
        for h in range(2):
            here.append(pltpu.make_async_copy(src(h, group[h]), dst(h, group[h]), loc.at[r, h]))
        return out, here

    def within(r, src, dst):
        out, here = [], []
        for d in ring:
            for h in range(2):
                t = lax.rem(spot[h] + d, 8)
                out.append(pltpu.make_async_remote_copy(
                    src_ref=src(h, t), dst_ref=dst(h, spot[h]),
                    send_sem=b_s.at[r, h, d - 1], recv_sem=b_r.at[r, h, d - 1],
                    device_id=device(h, group[h], t), device_id_type=MESH))
        for h in range(2):
            here.append(pltpu.make_async_copy(src(h, spot[h]), dst(h, spot[h]), loc.at[4 + r, h]))
        return out, here

    def rows_of(ref, k):
        def pick(h, b):
            if h == 0:
                return ref.at[k, :, lax.div(b, 2), lax.rem(b, 2), 0]
            return ref.at[k, lax.div(b, 2), :, lax.rem(b, 2), 1]

        return pick

    out_first = lambda: along(0, lambda h, a: sent.at[h, a, first], lambda h, a: mid.at[h, a, first])
    out_more = lambda: along(1, lambda h, a: sent.at[h, a, more], lambda h, a: mid.at[h, a, more])
    to_first = lambda: within(0, lambda h, b: mid.at[h, :, b], rows_of(held, 0))
    to_more = lambda k: within(k, lambda h, b: pad.at[k - 1, h, b], rows_of(held, k))
    arrive = lambda k: within(k, lambda h, b: pad.at[0, h, b], rows_of(held, k))
    from_slot = lambda k: within(3 + k, rows_of(back, k), lambda h, b: rmid.at[k, h, b])
    in_first = lambda: along(2, lambda h, a: rmid.at[0, h, :, a], lambda h, a: fin.at[h, a, first])
    in_more = lambda: along(3, lambda h, a: comp.at[h, a], lambda h, a: fin.at[h, a, more])

    def start(copies):
        for copy in copies[0] + copies[1]:
            copy.start()

    def landed(copies):
        for copy in copies[0]:
            copy.wait_recv()
        for copy in copies[1]:
            copy.wait()

    def gone(copies):
        for copy in copies[0]:
            copy.wait_send()

    for copy in fetches:
        copy.wait()
    lax.fori_loop(0, 32, build_first, 0, unroll=8)
    pl.semaphore_wait(barrier, 16)
    start(out_first())

    squares = lax.fori_loop(0, grad_ref.shape[1], square_sum, jnp.zeros((8, 128), F32), unroll=8)
    sums[0] = squares
    sum_copies = []

    def sum_send(stage, at, peers):
        copies = []
        for i, peer in enumerate(peers):
            copies.append(pltpu.make_async_remote_copy(
                src_ref=sums.at[stage], dst_ref=sumv.at[at + i],
                send_sem=sum_s.at[at + i], recv_sem=sum_r.at[at + i],
                device_id=peer, device_id_type=MESH))
        for copy in copies:
            copy.start()
        sum_copies.extend(copies)
        return copies

    def sum_take(stage, at, copies):
        acc = sums[stage]
        for i, copy in enumerate(copies):
            copy.wait_recv()
            acc = acc + sumv[at + i]
        sums[stage + 1] = acc

    s0 = sum_send(0, 0, [(lax.rem(e + d, 4), me) for d in range(1, 4)])
    fill_table(row_ref, table_v, row)
    lists = pltpu.make_async_copy(table_v, table_ref, io_in.at[3])
    lists.start()
    flags[0] = table_v[...].astype(F32)
    flag_copies = []
    for d in range(1, 4):
        flag_copies.append(pltpu.make_async_remote_copy(
            src_ref=flags.at[0], dst_ref=flags.at[d], send_sem=flag_s.at[d - 1], recv_sem=flag_r.at[d - 1],
            device_id=(lax.rem(e + d, 4), me), device_id_type=MESH))
    for copy in flag_copies:
        copy.start()
    lists.wait()
    lax.fori_loop(0, 4 * cap, build_more, 0, unroll=4)
    sum_take(0, 0, s0)
    s1 = sum_send(1, 3, [device(0, lax.rem(z + d, 4), spot[0]) for d in range(1, 4)])
    start(out_more())
    loads = [
        pltpu.make_async_copy(left_ref.at[0], lbuf, io_in.at[0]),
        pltpu.make_async_copy(right_ref.at[0], rbuf, io_in.at[1]),
    ]
    for copy in loads:
        copy.start()
    landed(out_first())
    sum_take(1, 3, s1)
    s2 = sum_send(2, 6, [device(0, z, lax.rem(spot[0] + d, 8)) for d in range(1, 8)])
    start(to_first())
    landed(out_more())
    build_pad(1)
    start(to_more(1))
    build_pad(2)
    start(to_more(2))
    sum_take(2, 6, s2)
    mean_square = total(sums[3]) / (4.0 * 32.0 * 512.0 * 512.0)
    factor = jnp.minimum(1.0, 1.0 / jnp.sqrt(mean_square + 1e-06))
    over = flags[0]
    for d, copy in enumerate(flag_copies):
        copy.wait_recv()
        over = over + flags[d + 1]
    over_ref[0, 0] = jnp.sum(over[OVER:OVER + 1, 0:1]).astype(jnp.int32)
    for copy in loads:
        copy.wait()

    def put(high, low, i, j, value):
        a, b = split(value)
        high[part(i), part(j)] = a
        low[part(i), part(j)] = b

    def both(high, low, i, j, value):
        put(high, low, i, j, value)
        if i != j:
            put(high, low, j, i, value.T)

    tiles = ((0, 0), (0, 1), (1, 1))

    def stat(n, buf, k, live, high, low):
        square = jnp.zeros((1, 1), F32)

        def take(i, j, product):
            old = buf[k, part(i), part(j)]
            new = 0.95 * old + product
            a_buf[n, part(i), part(j)] = new
            put(xh.at[n], xl.at[n], i, j, new)
            buf[k, part(i), part(j)] = jnp.where(live, new, old)
            return total(new * new)

        for i, j in tiles:
            one = low(i, j)
            other = one if i == j else low(j, i)
            product = high(i, j) + (one + other.T)
            square = square + take(i, j, product)
            if i != j:
                square = square + take(j, i, product.T)
        return square

    def second(n, inverse):
        for i, j in tiles:
            low = dot(xh[n, part(i), :], xl[n, :, part(j)])
            other = low if i == j else dot(xh[n, part(j), :], xl[n, :, part(i)])
            value = (dot(xh[n, part(i), :], xh[n, :, part(j)]) + (low + other.T)) * (inverse * inverse)
            base[n, part(i), part(j)] = value
            yh[n, part(i), part(j)] = value.astype(BF16)
            if i != j:
                yh[n, part(j), part(i)] = value.T.astype(BF16)

    def third(n, inverse):
        for i, j in tiles:
            x3 = (dot(yh[n, part(i), :], xh[n, :, part(j)]) + dot(yh[n, part(i), :], xl[n, :, part(j)])) * inverse
            x1 = a_buf[n, part(i), part(j)] * inverse
            x2 = base[n, part(i), part(j)]
            value = C1 * x1 + C2 * x2 + C3 * x3
            if i == j:
                rows = lax.broadcasted_iota(jnp.int32, (HALF, HALF), 0)
                cols = lax.broadcasted_iota(jnp.int32, (HALF, HALF), 1)
                value = value + jnp.where(rows == cols, C0, 0.0)
            base[n, part(i), part(j)] = value
            rest = C4 * x1 + C5 * x2 + C6 * x3
            oh[n, part(i), part(j)] = x3.astype(BF16)
            ol[n, part(i), part(j)] = rest.astype(BF16)
            if i != j:
                oh[n, part(j), part(i)] = x3.T.astype(BF16)
                ol[n, part(j), part(i)] = rest.T.astype(BF16)

    def last(n):
        for i, j in tiles:
            both(xh.at[n], xl.at[n], i, j, base[n, part(i), part(j)] + dot(oh[n, part(i), :], ol[n, :, part(j)]))

    def slot(k):
        live = assign_ref[0, me * 3 + k] >= 0
        graft = jnp.zeros((1, 1), F32)
        for i in range(2):
            for j in range(2):
                piece = held[k, 2 * i:2 * i + 2, :, :, :, :, part(j)].reshape(HALF, HALF) * factor
                graft = graft + total(piece * piece)
                put(sh, sl, i, j, piece)
        nt, tn = ((1,), (1,)), ((0,), (0,))
        squares = (
            stat(0, lbuf, k, live,
                 lambda i, j: dot(sh[part(i), :], sh[part(j), :], nt),
                 lambda i, j: dot(sh[part(i), :], sl[part(j), :], nt)),
            stat(1, rbuf, k, live,
                 lambda i, j: dot(sh[:, part(i)], sh[:, part(j)], tn),
                 lambda i, j: dot(sh[:, part(i)], sl[:, part(j)], tn)))
        norms = [jnp.sqrt(square + 1e-06) for square in squares]
        inverses = [1.0 / norm for norm in norms]
        for n in range(2):
            second(n, inverses[n])
        for n in range(2):
            third(n, inverses[n])
        for n in range(2):
            last(n)
        scale = 1.0 / (jnp.sqrt(jnp.sqrt(norms[0])) * jnp.sqrt(jnp.sqrt(norms[1])))

        th, tl = oh.at[0], ol.at[0]
        for i in range(2):
            for j in range(2):
                put(th, tl, i, j, dot(xh[0, part(i), :], sh[:, part(j)])
                    + (dot(xh[0, part(i), :], sl[:, part(j)]) + dot(xl[0, part(i), :], sh[:, part(j)])))
        square = jnp.zeros((1, 1), F32)
        for i in range(2):
            for j in range(2):
                value = dot(th[part(i), :], xh[1, :, part(j)]) + (
                    dot(th[part(i), :], xl[1, :, part(j)]) + dot(tl[part(i), :], xh[1, :, part(j)]))
                square = square + total(value * value)
                base[0, part(i), part(j)] = value
        count = 512.0 * 512.0
        ratio = scale * jnp.sqrt(graft / count + 1e-12) / jnp.sqrt(square * (scale * scale) / count + 1e-12)
        for i in range(2):
            back[k, 2 * i:2 * i + 2] = (base[0, part(i), :] * ratio).reshape(2, 4, 2, 2, 8, 512)

    def turn(k, carry):
        landed(arrive(k))
        slot(k)
        start(from_slot(k))
        return carry

    lax.fori_loop(0, 3, turn, 0)
    landed(from_slot(0))
    start(in_first())
    landed(from_slot(1))
    landed(from_slot(2))
    lax.fori_loop(0, cap, build_comp, 0, unroll=4)
    start(in_more())
    gone(out_first())
    gone(out_more())
    gone(to_first())
    gone(to_more(1))
    gone(to_more(2))
    for k in range(3):
        gone(from_slot(k))
    for copy in sum_copies + flag_copies:
        copy.wait_send()
    for copies in (in_first(), in_more()):
        landed(copies)
        gone(copies)

    def take(b, carry):
        s = look(OWNER, b, 95)
        _, za, xa, _, _ = place(s)
        for h, a in enumerate((za, xa)):
            entry = look(ENTRY_A + h, s, 7 + cap)
            update_ref[0, b, h * 8:h * 8 + 8] = fin[h, a, entry]
        return carry

    lax.fori_loop(0, update_ref.shape[1], take, 0, unroll=4)


def step(cap, ident, assign, gradient, left_stat, right_stat):
    vm = lambda *shape, dtype=F32: pltpu.VMEM(shape, dtype)
    half = lambda *shape: pltpu.VMEM(shape, BF16)
    dma = lambda *shape: pltpu.SemaphoreType.DMA(shape)
    any_spec = pl.BlockSpec(memory_space=pl.ANY)
    vmem = pl.BlockSpec(memory_space=pltpu.VMEM)
    entries = 8 + cap
    piece = (3, 4, 4, 2, 2, 8, 512)
    return pl.pallas_call(
        functools.partial(step_kernel, cap),
        out_shape=(
            jax.ShapeDtypeStruct(gradient.shape, F32),
            jax.ShapeDtypeStruct(left_stat.shape, F32),
            jax.ShapeDtypeStruct(right_stat.shape, F32),
            jax.ShapeDtypeStruct((1, 1), jnp.int32),
        ),
        in_specs=[any_spec] * 4,
        out_specs=(vmem, vmem, vmem, pl.BlockSpec(memory_space=pltpu.SMEM)),
        scratch_shapes=[
            vm(2, 4, entries, 8, 512), vm(2, 4, entries, 8, 512), vm(2, 2, 8, 4, 8, 512), vm(*piece),
            vm(*piece), vm(3, 2, 8, 4, 8, 512), vm(2, 4, cap, 8, 512), vm(2, 4, entries, 8, 512),
            pltpu.SMEM((1, 96), jnp.int32), vm(1, 96, dtype=jnp.int32), vm(1, 32, 16, 512), vm(4, 8, 128), vm(13, 8, 128), vm(4, 8, 128),
            vm(8, 128), vm(8, 128, dtype=jnp.int32), pltpu.SMEM((8, 128), jnp.int32),
            half(512, 512), half(512, 512), vm(2, 512, 512), vm(2, 512, 512),
            half(2, 512, 512), half(2, 512, 512), half(2, 512, 512), half(2, 512, 512), half(2, 512, 512),
            dma(4, 2, 3), dma(4, 2, 3), dma(6, 2, 7), dma(6, 2, 7), dma(10, 2), dma(13), dma(13), dma(3), dma(3),
            dma(6),
        ],
        name="step" + str(cap),
        compiler_params=pltpu.CompilerParams(collective_id=ident, has_side_effects=True, vmem_limit_bytes=(44 if cap == CAP else 63) * 2**20),
    )(assign, gradient, left_stat, right_stat)


def store_kernel(update_in, left_in, right_in, update_out, left_out, right_out):
    left_out[...] = left_in[...]
    right_out[...] = right_in[...]

    @pl.when(pl.program_id(0) == 0)
    def _():
        update_out[...] = update_in[...]


def store(outs):
    slot_spec = pl.BlockSpec((1, 1, 512, 512), lambda k: (0, k, 0, 0))
    whole = pl.BlockSpec((1, 32, 16, 512), lambda k: (0, 0, 0, 0))
    return pl.pallas_call(
        store_kernel,
        grid=(3,),
        out_shape=tuple(jax.ShapeDtypeStruct(out.shape, out.dtype) for out in outs),
        in_specs=[whole, slot_spec, slot_spec],
        out_specs=(whole, slot_spec, slot_spec),
        name="store",
        compiler_params=pltpu.CompilerParams(vmem_limit_bytes=30 * 2**20),
    )(*outs)


def body(gradient, left_stat, right_stat, assign):
    *outs, over = step(CAP, 0, assign, gradient, left_stat, right_stat)

    def again(_):
        return store(step(FULL, 1, assign, gradient, left_stat, right_stat)[:3])

    return lax.cond(over[0, 0] > 0, again, lambda kept: kept, store(outs))


def solution(mesh):
    placed = P("expert", None, "shard", None)
    slots = P("expert", "shard", None, None)
    return jax.shard_map(
        body,
        mesh=mesh,
        in_specs=(placed, slots, slots, P("expert", None)),
        out_specs=(placed, slots, slots),
        check_vma=False,
    )
```

```python
import functools

import jax
import jax.numpy as jnp
from jax import lax
from jax.experimental import pallas as pl
from jax.experimental.pallas import tpu as pltpu
from jax.sharding import PartitionSpec as P

MESH = pl.DeviceIdType.MESH
F32 = jnp.float32
BF16 = jnp.bfloat16
HALF = 256
CAP = 8
FULL = 16
LIST_A, LIST_B, OWNER, ENTRY_A, ENTRY_B, OVER = range(6)

C0 = 25.0 / 16.0
C1 = -5.0 / 16.0 - 3125.0 / 4096.0
C2 = 3125.0 / 4096.0
C3 = -1250.0 / 4096.0
C4 = 250.0 / 4096.0
C5 = -25.0 / 4096.0
C6 = 1.0 / 4096.0


def split(value):
    high = value.astype(BF16)
    return high, (value - high.astype(F32)).astype(BF16)


def dot(a, b, dims=((1,), (0,))):
    return lax.dot_general(a, b, (dims, ((), ())), preferred_element_type=F32)


def total(value):
    return jnp.sum(jnp.sum(value, axis=1, keepdims=True), axis=0, keepdims=True)


def part(i):
    return pl.ds(i * HALF, HALF)


def place(slot):
    d = (slot * 43) >> 7
    z, x, c = d >> 3, (d >> 1) & 3, d & 1
    return slot - 3 * d, z, x, d & 7, z * 2 + c


def fill_table(assign_ref, table_ref, row):
    shape = (128, 128)
    row[...] = jnp.full((8, 128), -1.0, F32)
    row[0:1, 0:96] = assign_ref[...].astype(F32)
    across = jnp.broadcast_to(row[0:1, :], shape)
    down = across.T
    i = lax.broadcasted_iota(jnp.int32, shape, 0)
    j = lax.broadcasted_iota(jnp.int32, shape, 1)
    rank_i, za_i, xa_i, _, _ = place(i)
    rank_j, za_j, xa_j, b0_j, b1_j = place(j)
    more_i = (down >= 0.0) & (rank_i > 0)
    more_j = (across >= 0.0) & (rank_j > 0)

    def count(mask, axis):
        return jnp.sum(jnp.where(mask, 1.0, 0.0), axis=axis, keepdims=True)

    over = jnp.zeros((1, 1), F32)
    for h, (ga_i, ga_j, b_j) in enumerate(((za_i, za_j, b0_j), (xa_i, xa_j, b1_j))):
        same = ga_i == ga_j
        before_i = count(more_j & same & (j < i), 1)
        before_j = count(more_i & same & (i < j), 0)
        listed = more_i & (ga_i == (j >> 4)) & (before_i == (j & 15).astype(F32))
        spots = jnp.sum(jnp.where(listed, i.astype(F32), 0.0), axis=0, keepdims=True)
        table_ref[LIST_A + h:LIST_A + h + 1, :] = jnp.minimum(spots, 95.0).astype(jnp.int32)
        entry = jnp.where(rank_j[0:1] == 0, b_j[0:1].astype(F32), 8.0 + before_j)
        table_ref[ENTRY_A + h:ENTRY_A + h + 1, :] = jnp.clip(entry, 0.0, 23.0).astype(jnp.int32)
        over = over + count(more_j[0:1] & (before_j >= float(CAP)), 1)
    owner = jnp.sum(jnp.where(down == j.astype(F32), i.astype(F32), 0.0), axis=0, keepdims=True)
    table_ref[OWNER:OWNER + 1, :] = jnp.minimum(owner, 95.0).astype(jnp.int32)
    table_ref[OVER:OVER + 1, :] = jnp.broadcast_to(over, (1, 128)).astype(jnp.int32)
    table_ref[OVER + 1:8, :] = jnp.zeros((7 - OVER, 128), jnp.int32)


def step_kernel(
    cap,
    slots_ref, gradient_ref, left_ref, right_ref,
    update_ref, new_left_ref, new_right_ref, over_ref,
    sent, mid, pad, held, back, rmid, comp, fin,
    assign_ref, row_ref, grad_ref, sums, sumv, flags, row, table_v, table_ref,
    sh, sl, a_buf, base, xh, xl, yh, oh, ol,
    a_s, a_r, b_s, b_r, loc, sum_s, sum_r, flag_s, flag_r, io_in,
):
    e = lax.axis_index("expert")
    me = lax.axis_index("shard")
    z, x, c = lax.div(me, 8), lax.rem(lax.div(me, 2), 4), lax.rem(me, 2)
    lbuf, rbuf = new_left_ref.at[0], new_right_ref.at[0]
    group = (z, x)
    spot = (x * 2 + c, z * 2 + c)

    def device(h, a, b):
        if h == 0:
            return (e, a * 8 + b)
        return (e, lax.div(b, 2) * 8 + a * 2 + lax.rem(b, 2))

    def index(h, a, b):
        return device(h, a, b)[1]

    fetches = [
        pltpu.make_async_copy(slots_ref, assign_ref, io_in.at[4]),
        pltpu.make_async_copy(gradient_ref, grad_ref, io_in.at[2]),
        pltpu.make_async_copy(slots_ref, row_ref, io_in.at[5]),
    ]
    for copy in fetches:
        copy.start()
    barrier = pltpu.get_barrier_semaphore()
    for d in range(1, 8):
        pl.semaphore_signal(barrier, inc=1, device_id=device(0, z, lax.rem(spot[0] + d, 8)), device_id_type=MESH)
    for d in range(1, 4):
        for f in range(2):
            pl.semaphore_signal(
                barrier, inc=1, device_id=(e, lax.rem(z + d, 4) * 8 + x * 2 + lax.rem(c + f, 2)), device_id_type=MESH)
    for d in range(1, 4):
        pl.semaphore_signal(barrier, inc=1, device_id=(lax.rem(e + d, 4), me), device_id_type=MESH)

    def square_sum(b, acc):
        rows = grad_ref[0, b]
        sq = rows * rows
        for q in range(4):
            acc = acc + sq[0:8, q * 128:(q + 1) * 128] + sq[8:16, q * 128:(q + 1) * 128]
        return acc


    def look(line, at, top):
        return jnp.clip(table_ref[line, at], 0, top)

    def build_first(d, carry):
        block = jnp.clip(assign_ref[0, d * 3], 0, 31)
        rows = grad_ref[0, block]
        zd, xd, cd = lax.div(d, 8), lax.rem(lax.div(d, 2), 4), lax.rem(d, 2)
        sent[0, zd, xd * 2 + cd] = rows[0:8]
        sent[1, xd, zd * 2 + cd] = rows[8:16]
        return carry

    def build_more(n, carry):
        a, j = lax.div(n, cap), lax.rem(n, cap)
        for h in range(2):
            block = jnp.clip(assign_ref[0, look(LIST_A + h, a * 16 + j, 95)], 0, 31)
            sent[h, a, 8 + j] = grad_ref[0, block, h * 8:h * 8 + 8]
        return carry

    def build_pad(k):
        def one(b, carry):
            for h in range(2):
                entry = look(ENTRY_A + h, index(h, group[h], b) * 3 + k, 7 + cap)
                pad[k - 1, h, b] = mid[h, :, entry]
            return carry

        lax.fori_loop(0, 8, one, 0, unroll=4)

    def build_comp(j, carry):
        for h in range(2):
            rank, _, _, b0, b1 = place(look(LIST_A + h, group[h] * 16 + j, 95))
            comp[h, :, j] = rmid[rank, h, (b0, b1)[h]]
        return carry

    first, more = pl.ds(0, 8), pl.ds(8, cap)
    near, ring = (2, 1, 3), (4, 3, 5, 2, 6, 1, 7)

    def along(r, src, dst):
        out, here = [], []
        for d in near:
            for h in range(2):
                t = lax.rem(group[h] + d, 4)
                out.append(pltpu.make_async_remote_copy(
                    src_ref=src(h, t), dst_ref=dst(h, group[h]),
                    send_sem=a_s.at[r, h, d - 1], recv_sem=a_r.at[r, h, d - 1],
                    device_id=device(h, t, spot[h]), device_id_type=MESH))
        for h in range(2):
            here.append(pltpu.make_async_copy(src(h, group[h]), dst(h, group[h]), loc.at[r, h]))
        return out, here

    def within(r, src, dst):
        out, here = [], []
        for d in ring:
            for h in range(2):
                t = lax.rem(spot[h] + d, 8)
                out.append(pltpu.make_async_remote_copy(
                    src_ref=src(h, t), dst_ref=dst(h, spot[h]),
                    send_sem=b_s.at[r, h, d - 1], recv_sem=b_r.at[r, h, d - 1],
                    device_id=device(h, group[h], t), device_id_type=MESH))
        for h in range(2):
            here.append(pltpu.make_async_copy(src(h, spot[h]), dst(h, spot[h]), loc.at[4 + r, h]))
        return out, here

    def rows_of(ref, k):
        def pick(h, b):
            if h == 0:
                return ref.at[k, :, lax.div(b, 2), lax.rem(b, 2), 0]
            return ref.at[k, lax.div(b, 2), :, lax.rem(b, 2), 1]

        return pick

    out_first = lambda: along(0, lambda h, a: sent.at[h, a, first], lambda h, a: mid.at[h, a, first])
    out_more = lambda: along(1, lambda h, a: sent.at[h, a, more], lambda h, a: mid.at[h, a, more])
    to_first = lambda: within(0, lambda h, b: mid.at[h, :, b], rows_of(held, 0))
    to_more = lambda k: within(k, lambda h, b: pad.at[k - 1, h, b], rows_of(held, k))
    arrive = lambda k: within(k, lambda h, b: pad.at[0, h, b], rows_of(held, k))
    from_slot = lambda k: within(3 + k, rows_of(back, k), lambda h, b: rmid.at[k, h, b])
    in_first = lambda: along(2, lambda h, a: rmid.at[0, h, :, a], lambda h, a: fin.at[h, a, first])
    in_more = lambda: along(3, lambda h, a: comp.at[h, a], lambda h, a: fin.at[h, a, more])

    def start(copies):
        for copy in copies[0] + copies[1]:
            copy.start()

    def landed(copies):
        for copy in copies[0]:
            copy.wait_recv()
        for copy in copies[1]:
            copy.wait()

    def gone(copies):
        for copy in copies[0]:
            copy.wait_send()

    for copy in fetches:
        copy.wait()
    lax.fori_loop(0, 32, build_first, 0, unroll=16)
    pl.semaphore_wait(barrier, 16)
    start(out_first())

    squares = lax.fori_loop(0, grad_ref.shape[1], square_sum, jnp.zeros((8, 128), F32), unroll=8)
    sums[0] = squares
    sum_copies = []

    def sum_send(stage, at, peers):
        copies = []
        for i, peer in enumerate(peers):
            copies.append(pltpu.make_async_remote_copy(
                src_ref=sums.at[stage], dst_ref=sumv.at[at + i],
                send_sem=sum_s.at[at + i], recv_sem=sum_r.at[at + i],
                device_id=peer, device_id_type=MESH))
        for copy in copies:
            copy.start()
        sum_copies.extend(copies)
        return copies

    def sum_take(stage, at, copies):
        acc = sums[stage]
        for i, copy in enumerate(copies):
            copy.wait_recv()
            acc = acc + sumv[at + i]
        sums[stage + 1] = acc

    s0 = sum_send(0, 0, [(lax.rem(e + d, 4), me) for d in range(1, 4)])
    fill_table(row_ref, table_v, row)
    lists = pltpu.make_async_copy(table_v, table_ref, io_in.at[3])
    lists.start()
    flags[0] = table_v[...].astype(F32)
    flag_copies = []
    for d in range(1, 4):
        flag_copies.append(pltpu.make_async_remote_copy(
            src_ref=flags.at[0], dst_ref=flags.at[d], send_sem=flag_s.at[d - 1], recv_sem=flag_r.at[d - 1],
            device_id=(lax.rem(e + d, 4), me), device_id_type=MESH))
    for copy in flag_copies:
        copy.start()
    lists.wait()
    lax.fori_loop(0, 4 * cap, build_more, 0, unroll=4)
    sum_take(0, 0, s0)
    s1 = sum_send(1, 3, [device(0, lax.rem(z + d, 4), spot[0]) for d in range(1, 4)])
    start(out_more())
    loads = [
        pltpu.make_async_copy(left_ref.at[0], lbuf, io_in.at[0]),
        pltpu.make_async_copy(right_ref.at[0], rbuf, io_in.at[1]),
    ]
    for copy in loads:
        copy.start()
    landed(out_first())
    sum_take(1, 3, s1)
    s2 = sum_send(2, 6, [device(0, z, lax.rem(spot[0] + d, 8)) for d in range(1, 8)])
    start(to_first())
    landed(out_more())
    build_pad(1)
    start(to_more(1))
    build_pad(2)
    start(to_more(2))
    sum_take(2, 6, s2)
    mean_square = total(sums[3]) / (4.0 * 32.0 * 512.0 * 512.0)
    factor = jnp.minimum(1.0, 1.0 / jnp.sqrt(mean_square + 1e-06))
    over = flags[0]
    for d, copy in enumerate(flag_copies):
        copy.wait_recv()
        over = over + flags[d + 1]
    over_ref[0, 0] = jnp.sum(over[OVER:OVER + 1, 0:1]).astype(jnp.int32)
    for copy in loads:
        copy.wait()

    def put(high, low, i, j, value):
        a, b = split(value)
        high[part(i), part(j)] = a
        low[part(i), part(j)] = b

    def both(high, low, i, j, value):
        put(high, low, i, j, value)
        if i != j:
            put(high, low, j, i, value.T)

    tiles = ((0, 0), (0, 1), (1, 1))

    def stat(n, buf, k, live, high, low):
        square = jnp.zeros((1, 1), F32)

        def take(i, j, product):
            old = buf[k, part(i), part(j)]
            new = 0.95 * old + product
            a_buf[n, part(i), part(j)] = new
            put(xh.at[n], xl.at[n], i, j, new)
            buf[k, part(i), part(j)] = jnp.where(live, new, old)
            return total(new * new)

        for i, j in tiles:
            one = low(i, j)
            other = one if i == j else low(j, i)
            product = high(i, j) + (one + other.T)
            square = square + take(i, j, product)
            if i != j:
                square = square + take(j, i, product.T)
        return square

    def second(n, inverse):
        for i, j in tiles:
            low = dot(xh[n, part(i), :], xl[n, :, part(j)])
            other = low if i == j else dot(xh[n, part(j), :], xl[n, :, part(i)])
            value = (dot(xh[n, part(i), :], xh[n, :, part(j)]) + (low + other.T)) * inverse * inverse
            base[n, part(i), part(j)] = value
            yh[n, part(i), part(j)] = value.astype(BF16)
            if i != j:
                yh[n, part(j), part(i)] = value.T.astype(BF16)

    def third(n, inverse):
        for i, j in tiles:
            x3 = (dot(yh[n, part(i), :], xh[n, :, part(j)]) + dot(yh[n, part(i), :], xl[n, :, part(j)])) * inverse
            x1 = a_buf[n, part(i), part(j)] * inverse
            x2 = base[n, part(i), part(j)]
            value = C1 * x1 + C2 * x2 + C3 * x3
            if i == j:
                rows = lax.broadcasted_iota(jnp.int32, (HALF, HALF), 0)
                cols = lax.broadcasted_iota(jnp.int32, (HALF, HALF), 1)
                value = value + jnp.where(rows == cols, C0, 0.0)
            base[n, part(i), part(j)] = value
            rest = C4 * x1 + C5 * x2 + C6 * x3
            oh[n, part(i), part(j)] = x3.astype(BF16)
            ol[n, part(i), part(j)] = rest.astype(BF16)
            if i != j:
                oh[n, part(j), part(i)] = x3.T.astype(BF16)
                ol[n, part(j), part(i)] = rest.T.astype(BF16)

    def last(n):
        for i, j in tiles:
            both(xh.at[n], xl.at[n], i, j, base[n, part(i), part(j)] + dot(oh[n, part(i), :], ol[n, :, part(j)]))

    def slot(k):
        live = assign_ref[0, me * 3 + k] >= 0
        graft = jnp.zeros((1, 1), F32)
        for i in range(2):
            for j in range(2):
                piece = held[k, 2 * i:2 * i + 2, :, :, :, :, part(j)].reshape(HALF, HALF) * factor
                graft = graft + total(piece * piece)
                put(sh, sl, i, j, piece)
        nt, tn = ((1,), (1,)), ((0,), (0,))
        squares = (
            stat(0, lbuf, k, live,
                 lambda i, j: dot(sh[part(i), :], sh[part(j), :], nt),
                 lambda i, j: dot(sh[part(i), :], sl[part(j), :], nt)),
            stat(1, rbuf, k, live,
                 lambda i, j: dot(sh[:, part(i)], sh[:, part(j)], tn),
                 lambda i, j: dot(sh[:, part(i)], sl[:, part(j)], tn)))
        norms = [jnp.sqrt(square + 1e-06) for square in squares]
        inverses = [1.0 / norm for norm in norms]
        for n in range(2):
            second(n, inverses[n])
        for n in range(2):
            third(n, inverses[n])
        for n in range(2):
            last(n)
        scale = 1.0 / (jnp.sqrt(jnp.sqrt(norms[0])) * jnp.sqrt(jnp.sqrt(norms[1])))

        th, tl = oh.at[0], ol.at[0]
        for i in range(2):
            for j in range(2):
                put(th, tl, i, j, dot(xh[0, part(i), :], sh[:, part(j)])
                    + (dot(xh[0, part(i), :], sl[:, part(j)]) + dot(xl[0, part(i), :], sh[:, part(j)])))
        square = jnp.zeros((1, 1), F32)
        for i in range(2):
            for j in range(2):
                value = dot(th[part(i), :], xh[1, :, part(j)]) + (
                    dot(th[part(i), :], xl[1, :, part(j)]) + dot(tl[part(i), :], xh[1, :, part(j)]))
                square = square + total(value * value)
                base[0, part(i), part(j)] = value
        count = 512.0 * 512.0
        ratio = scale * jnp.sqrt(graft / count + 1e-12) / jnp.sqrt(square * (scale * scale) / count + 1e-12)
        for i in range(2):
            back[k, 2 * i:2 * i + 2] = (base[0, part(i), :] * ratio).reshape(2, 4, 2, 2, 8, 512)

    def turn(k, carry):
        landed(arrive(k))
        slot(k)
        start(from_slot(k))
        return carry

    lax.fori_loop(0, 3, turn, 0)
    landed(from_slot(0))
    start(in_first())
    landed(from_slot(1))
    landed(from_slot(2))
    lax.fori_loop(0, cap, build_comp, 0, unroll=8)
    start(in_more())
    gone(out_first())
    gone(out_more())
    gone(to_first())
    gone(to_more(1))
    gone(to_more(2))
    for k in range(3):
        gone(from_slot(k))
    for copy in sum_copies + flag_copies:
        copy.wait_send()
    for copies in (in_first(), in_more()):
        landed(copies)
        gone(copies)

    def take(b, carry):
        s = look(OWNER, b, 95)
        _, za, xa, _, _ = place(s)
        for h, a in enumerate((za, xa)):
            entry = look(ENTRY_A + h, s, 7 + cap)
            update_ref[0, b, h * 8:h * 8 + 8] = fin[h, a, entry]
        return carry

    lax.fori_loop(0, update_ref.shape[1], take, 0, unroll=16)


def step(cap, ident, assign, gradient, left_stat, right_stat):
    vm = lambda *shape, dtype=F32: pltpu.VMEM(shape, dtype)
    half = lambda *shape: pltpu.VMEM(shape, BF16)
    dma = lambda *shape: pltpu.SemaphoreType.DMA(shape)
    any_spec = pl.BlockSpec(memory_space=pl.ANY)
    vmem = pl.BlockSpec(memory_space=pltpu.VMEM)
    entries = 8 + cap
    piece = (3, 4, 4, 2, 2, 8, 512)
    return pl.pallas_call(
        functools.partial(step_kernel, cap),
        out_shape=(
            jax.ShapeDtypeStruct(gradient.shape, F32),
            jax.ShapeDtypeStruct(left_stat.shape, F32),
            jax.ShapeDtypeStruct(right_stat.shape, F32),
            jax.ShapeDtypeStruct((1, 1), jnp.int32),
        ),
        in_specs=[any_spec] * 4,
        out_specs=(vmem, vmem, vmem, pl.BlockSpec(memory_space=pltpu.SMEM)),
        scratch_shapes=[
            vm(2, 4, entries, 8, 512), vm(2, 4, entries, 8, 512), vm(2, 2, 8, 4, 8, 512), vm(*piece),
            vm(*piece), vm(3, 2, 8, 4, 8, 512), vm(2, 4, cap, 8, 512), vm(2, 4, entries, 8, 512),
            pltpu.SMEM((1, 96), jnp.int32), vm(1, 96, dtype=jnp.int32), vm(1, 32, 16, 512), vm(4, 8, 128), vm(13, 8, 128), vm(4, 8, 128),
            vm(8, 128), vm(8, 128, dtype=jnp.int32), pltpu.SMEM((8, 128), jnp.int32),
            half(512, 512), half(512, 512), vm(2, 512, 512), vm(2, 512, 512),
            half(2, 512, 512), half(2, 512, 512), half(2, 512, 512), half(2, 512, 512), half(2, 512, 512),
            dma(4, 2, 3), dma(4, 2, 3), dma(6, 2, 7), dma(6, 2, 7), dma(10, 2), dma(13), dma(13), dma(3), dma(3),
            dma(6),
        ],
        name="step" + str(cap),
        compiler_params=pltpu.CompilerParams(collective_id=ident, has_side_effects=True, vmem_limit_bytes=(44 if cap == CAP else 63) * 2**20),
    )(assign, gradient, left_stat, right_stat)


def store_kernel(update_in, left_in, right_in, update_out, left_out, right_out):
    left_out[...] = left_in[...]
    right_out[...] = right_in[...]

    @pl.when(pl.program_id(0) == 0)
    def _():
        update_out[...] = update_in[...]


def store(outs):
    slot_spec = pl.BlockSpec((1, 1, 512, 512), lambda k: (0, k, 0, 0))
    whole = pl.BlockSpec((1, 32, 16, 512), lambda k: (0, 0, 0, 0))
    return pl.pallas_call(
        store_kernel,
        grid=(3,),
        out_shape=tuple(jax.ShapeDtypeStruct(out.shape, out.dtype) for out in outs),
        in_specs=[whole, slot_spec, slot_spec],
        out_specs=(whole, slot_spec, slot_spec),
        name="store",
        compiler_params=pltpu.CompilerParams(vmem_limit_bytes=30 * 2**20),
    )(*outs)


def body(gradient, left_stat, right_stat, assign):
    *outs, over = step(CAP, 0, assign, gradient, left_stat, right_stat)

    def again(_):
        return store(step(FULL, 1, assign, gradient, left_stat, right_stat)[:3])

    return lax.cond(over[0, 0] > 0, again, lambda kept: kept, store(outs))


def solution(mesh):
    placed = P("expert", None, "shard", None)
    slots = P("expert", "shard", None, None)
    return jax.shard_map(
        body,
        mesh=mesh,
        in_specs=(placed, slots, slots, P("expert", None)),
        out_specs=(placed, slots, slots),
        check_vma=False,
    )
```

```python
import functools

import jax
import jax.numpy as jnp
from jax import lax
from jax.experimental import pallas as pl
from jax.experimental.pallas import tpu as pltpu
from jax.sharding import PartitionSpec as P

MESH = pl.DeviceIdType.MESH
F32 = jnp.float32
BF16 = jnp.bfloat16
HALF = 256
CAP = 8
FULL = 16
LIST_A, LIST_B, OWNER, ENTRY_A, ENTRY_B, OVER = range(6)

C0 = 25.0 / 16.0
C1 = -5.0 / 16.0 - 3125.0 / 4096.0
C2 = 3125.0 / 4096.0
C3 = -1250.0 / 4096.0
C4 = 250.0 / 4096.0
C5 = -25.0 / 4096.0
C6 = 1.0 / 4096.0


def split(value):
    high = value.astype(BF16)
    return high, (value - high.astype(F32)).astype(BF16)


def dot(a, b, dims=((1,), (0,))):
    return lax.dot_general(a, b, (dims, ((), ())), preferred_element_type=F32)


def total(value):
    return jnp.sum(jnp.sum(value, axis=1, keepdims=True), axis=0, keepdims=True)


def part(i):
    return pl.ds(i * HALF, HALF)


def place(slot):
    d = (slot * 43) >> 7
    z, x, c = d >> 3, (d >> 1) & 3, d & 1
    return slot - 3 * d, z, x, d & 7, z * 2 + c


def fill_table(assign_ref, table_ref, row):
    shape = (128, 128)
    row[...] = jnp.full((8, 128), -1.0, F32)
    row[0:1, 0:96] = assign_ref[...].astype(F32)
    across = jnp.broadcast_to(row[0:1, :], shape)
    down = across.T
    i = lax.broadcasted_iota(jnp.int32, shape, 0)
    j = lax.broadcasted_iota(jnp.int32, shape, 1)
    rank_i, za_i, xa_i, _, _ = place(i)
    rank_j, za_j, xa_j, b0_j, b1_j = place(j)
    more_i = (down >= 0.0) & (rank_i > 0)
    more_j = (across >= 0.0) & (rank_j > 0)

    def count(mask, axis):
        return jnp.sum(jnp.where(mask, 1.0, 0.0), axis=axis, keepdims=True)

    over = jnp.zeros((1, 1), F32)
    for h, (ga_i, ga_j, b_j) in enumerate(((za_i, za_j, b0_j), (xa_i, xa_j, b1_j))):
        same = ga_i == ga_j
        before_i = count(more_j & same & (j < i), 1)
        before_j = count(more_i & same & (i < j), 0)
        listed = more_i & (ga_i == (j >> 4)) & (before_i == (j & 15).astype(F32))
        spots = jnp.sum(jnp.where(listed, i.astype(F32), 0.0), axis=0, keepdims=True)
        table_ref[LIST_A + h:LIST_A + h + 1, :] = jnp.minimum(spots, 95.0).astype(jnp.int32)
        entry = jnp.where(rank_j[0:1] == 0, b_j[0:1].astype(F32), 8.0 + before_j)
        table_ref[ENTRY_A + h:ENTRY_A + h + 1, :] = jnp.clip(entry, 0.0, 23.0).astype(jnp.int32)
        over = over + count(more_j[0:1] & (before_j >= float(CAP)), 1)
    owner = jnp.sum(jnp.where(down == j.astype(F32), i.astype(F32), 0.0), axis=0, keepdims=True)
    table_ref[OWNER:OWNER + 1, :] = jnp.minimum(owner, 95.0).astype(jnp.int32)
    table_ref[OVER:OVER + 1, :] = jnp.broadcast_to(over, (1, 128)).astype(jnp.int32)
    table_ref[OVER + 1:8, :] = jnp.zeros((7 - OVER, 128), jnp.int32)


def step_kernel(
    cap,
    slots_ref, gradient_ref, left_ref, right_ref,
    update_ref, new_left_ref, new_right_ref, over_ref,
    sent, mid, pad, held, back, rmid, comp, fin,
    assign_ref, row_ref, grad_ref, sums, sumv, flags, row, table_v, table_ref,
    sh, sl, a_buf, base, xh, xl, yh, oh, ol,
    a_s, a_r, b_s, b_r, loc, sum_s, sum_r, flag_s, flag_r, io_in,
):
    e = lax.axis_index("expert")
    me = lax.axis_index("shard")
    z, x, c = lax.div(me, 8), lax.rem(lax.div(me, 2), 4), lax.rem(me, 2)
    lbuf, rbuf = new_left_ref.at[0], new_right_ref.at[0]
    group = (z, x)
    spot = (x * 2 + c, z * 2 + c)

    def device(h, a, b):
        if h == 0:
            return (e, a * 8 + b)
        return (e, lax.div(b, 2) * 8 + a * 2 + lax.rem(b, 2))

    def index(h, a, b):
        return device(h, a, b)[1]

    fetches = [
        pltpu.make_async_copy(slots_ref, assign_ref, io_in.at[4]),
        pltpu.make_async_copy(gradient_ref, grad_ref, io_in.at[2]),
        pltpu.make_async_copy(slots_ref, row_ref, io_in.at[5]),
    ]
    for copy in fetches:
        copy.start()
    barrier = pltpu.get_barrier_semaphore()
    for d in range(1, 8):
        pl.semaphore_signal(barrier, inc=1, device_id=device(0, z, lax.rem(spot[0] + d, 8)), device_id_type=MESH)
    for d in range(1, 4):
        for f in range(2):
            pl.semaphore_signal(
                barrier, inc=1, device_id=(e, lax.rem(z + d, 4) * 8 + x * 2 + lax.rem(c + f, 2)), device_id_type=MESH)
    for d in range(1, 4):
        pl.semaphore_signal(barrier, inc=1, device_id=(lax.rem(e + d, 4), me), device_id_type=MESH)

    def square_sum(b, acc):
        rows = grad_ref[0, b]
        sq = rows * rows
        for q in range(4):
            acc = acc + sq[0:8, q * 128:(q + 1) * 128] + sq[8:16, q * 128:(q + 1) * 128]
        return acc


    def look(line, at, top):
        return jnp.clip(table_ref[line, at], 0, top)

    def build_first(d, carry):
        block = jnp.clip(assign_ref[0, d * 3], 0, 31)
        rows = grad_ref[0, block]
        zd, xd, cd = lax.div(d, 8), lax.rem(lax.div(d, 2), 4), lax.rem(d, 2)
        sent[0, zd, xd * 2 + cd] = rows[0:8]
        sent[1, xd, zd * 2 + cd] = rows[8:16]
        return carry

    def build_more(n, carry):
        a, j = lax.div(n, cap), lax.rem(n, cap)
        for h in range(2):
            block = jnp.clip(assign_ref[0, look(LIST_A + h, a * 16 + j, 95)], 0, 31)
            sent[h, a, 8 + j] = grad_ref[0, block, h * 8:h * 8 + 8]
        return carry

    def build_pad(k):
        def one(b, carry):
            for h in range(2):
                entry = look(ENTRY_A + h, index(h, group[h], b) * 3 + k, 7 + cap)
                pad[k - 1, h, b] = mid[h, :, entry]
            return carry

        lax.fori_loop(0, 8, one, 0, unroll=4)

    def build_comp(j, carry):
        for h in range(2):
            rank, _, _, b0, b1 = place(look(LIST_A + h, group[h] * 16 + j, 95))
            comp[h, :, j] = rmid[rank, h, (b0, b1)[h]]
        return carry

    first, more = pl.ds(0, 8), pl.ds(8, cap)
    near, ring = (2, 1, 3), (4, 3, 5, 2, 6, 1, 7)

    def along(r, src, dst):
        out, here = [], []
        for d in near:
            for h in range(2):
                t = lax.rem(group[h] + d, 4)
                out.append(pltpu.make_async_remote_copy(
                    src_ref=src(h, t), dst_ref=dst(h, group[h]),
                    send_sem=a_s.at[r, h, d - 1], recv_sem=a_r.at[r, h, d - 1],
                    device_id=device(h, t, spot[h]), device_id_type=MESH))
        for h in range(2):
            here.append(pltpu.make_async_copy(src(h, group[h]), dst(h, group[h]), loc.at[r, h]))
        return out, here

    def within(r, src, dst):
        out, here = [], []
        for d in ring:
            for h in range(2):
                t = lax.rem(spot[h] + d, 8)
                out.append(pltpu.make_async_remote_copy(
                    src_ref=src(h, t), dst_ref=dst(h, spot[h]),
                    send_sem=b_s.at[r, h, d - 1], recv_sem=b_r.at[r, h, d - 1],
                    device_id=device(h, group[h], t), device_id_type=MESH))
        for h in range(2):
            here.append(pltpu.make_async_copy(src(h, spot[h]), dst(h, spot[h]), loc.at[4 + r, h]))
        return out, here

    def rows_of(ref, k):
        def pick(h, b):
            if h == 0:
                return ref.at[k, :, lax.div(b, 2), lax.rem(b, 2), 0]
            return ref.at[k, lax.div(b, 2), :, lax.rem(b, 2), 1]

        return pick

    out_first = lambda: along(0, lambda h, a: sent.at[h, a, first], lambda h, a: mid.at[h, a, first])
    out_more = lambda: along(1, lambda h, a: sent.at[h, a, more], lambda h, a: mid.at[h, a, more])
    to_first = lambda: within(0, lambda h, b: mid.at[h, :, b], rows_of(held, 0))
    to_more = lambda k: within(k, lambda h, b: pad.at[k - 1, h, b], rows_of(held, k))
    arrive = lambda k: within(k, lambda h, b: pad.at[0, h, b], rows_of(held, k))
    from_slot = lambda k: within(3 + k, rows_of(back, k), lambda h, b: rmid.at[k, h, b])
    in_first = lambda: along(2, lambda h, a: rmid.at[0, h, :, a], lambda h, a: fin.at[h, a, first])
    in_more = lambda: along(3, lambda h, a: comp.at[h, a], lambda h, a: fin.at[h, a, more])

    def start(copies):
        for copy in copies[0] + copies[1]:
            copy.start()

    def landed(copies):
        for copy in copies[0]:
            copy.wait_recv()
        for copy in copies[1]:
            copy.wait()

    def gone(copies):
        for copy in copies[0]:
            copy.wait_send()

    for copy in fetches:
        copy.wait()
    firsts, kept = out_first()
    for n, d in enumerate(near + (0,)):
        t = lax.rem(z + d, 4)
        lax.fori_loop(t * 8, t * 8 + 8, build_first, 0)
        if n == 0:
            pl.semaphore_wait(barrier, 16)
        if d:
            firsts[2 * n].start()
    for copy in firsts[1::2] + kept:
        copy.start()

    squares = lax.fori_loop(0, grad_ref.shape[1], square_sum, jnp.zeros((8, 128), F32), unroll=8)
    sums[0] = squares
    sum_copies = []

    def sum_send(stage, at, peers):
        copies = []
        for i, peer in enumerate(peers):
            copies.append(pltpu.make_async_remote_copy(
                src_ref=sums.at[stage], dst_ref=sumv.at[at + i],
                send_sem=sum_s.at[at + i], recv_sem=sum_r.at[at + i],
                device_id=peer, device_id_type=MESH))
        for copy in copies:
            copy.start()
        sum_copies.extend(copies)
        return copies

    def sum_take(stage, at, copies):
        acc = sums[stage]
        for i, copy in enumerate(copies):
            copy.wait_recv()
            acc = acc + sumv[at + i]
        sums[stage + 1] = acc

    s0 = sum_send(0, 0, [(lax.rem(e + d, 4), me) for d in range(1, 4)])
    fill_table(row_ref, table_v, row)
    lists = pltpu.make_async_copy(table_v, table_ref, io_in.at[3])
    lists.start()
    flags[0] = table_v[...].astype(F32)
    flag_copies = []
    for d in range(1, 4):
        flag_copies.append(pltpu.make_async_remote_copy(
            src_ref=flags.at[0], dst_ref=flags.at[d], send_sem=flag_s.at[d - 1], recv_sem=flag_r.at[d - 1],
            device_id=(lax.rem(e + d, 4), me), device_id_type=MESH))
    for copy in flag_copies:
        copy.start()
    lists.wait()
    lax.fori_loop(0, 4 * cap, build_more, 0, unroll=4)
    sum_take(0, 0, s0)
    s1 = sum_send(1, 3, [device(0, lax.rem(z + d, 4), spot[0]) for d in range(1, 4)])
    start(out_more())
    loads = [
        pltpu.make_async_copy(left_ref.at[0], lbuf, io_in.at[0]),
        pltpu.make_async_copy(right_ref.at[0], rbuf, io_in.at[1]),
    ]
    for copy in loads:
        copy.start()
    landed(out_first())
    sum_take(1, 3, s1)
    s2 = sum_send(2, 6, [device(0, z, lax.rem(spot[0] + d, 8)) for d in range(1, 8)])
    start(to_first())
    landed(out_more())
    build_pad(1)
    start(to_more(1))
    build_pad(2)
    start(to_more(2))
    sum_take(2, 6, s2)
    mean_square = total(sums[3]) / (4.0 * 32.0 * 512.0 * 512.0)
    factor = jnp.minimum(1.0, 1.0 / jnp.sqrt(mean_square + 1e-06))
    over = flags[0]
    for d, copy in enumerate(flag_copies):
        copy.wait_recv()
        over = over + flags[d + 1]
    over_ref[0, 0] = jnp.sum(over[OVER:OVER + 1, 0:1]).astype(jnp.int32)
    for copy in loads:
        copy.wait()

    def put(high, low, i, j, value):
        a, b = split(value)
        high[part(i), part(j)] = a
        low[part(i), part(j)] = b

    def both(high, low, i, j, value):
        put(high, low, i, j, value)
        if i != j:
            put(high, low, j, i, value.T)

    tiles = ((0, 0), (0, 1), (1, 1))

    def stat(n, buf, k, live, high, low):
        square = jnp.zeros((1, 1), F32)

        def take(i, j, product):
            old = buf[k, part(i), part(j)]
            new = 0.95 * old + product
            a_buf[n, part(i), part(j)] = new
            put(xh.at[n], xl.at[n], i, j, new)
            buf[k, part(i), part(j)] = jnp.where(live, new, old)
            return total(new * new)

        for i, j in tiles:
            one = low(i, j)
            other = one if i == j else low(j, i)
            product = high(i, j) + (one + other.T)
            square = square + take(i, j, product)
            if i != j:
                square = square + take(j, i, product.T)
        return square

    def second(n, inverse):
        for i, j in tiles:
            low = dot(xh[n, part(i), :], xl[n, :, part(j)])
            other = low if i == j else dot(xh[n, part(j), :], xl[n, :, part(i)])
            value = (dot(xh[n, part(i), :], xh[n, :, part(j)]) + (low + other.T)) * inverse * inverse
            base[n, part(i), part(j)] = value
            yh[n, part(i), part(j)] = value.astype(BF16)
            if i != j:
                yh[n, part(j), part(i)] = value.T.astype(BF16)

    def third(n, inverse):
        for i, j in tiles:
            x3 = (dot(yh[n, part(i), :], xh[n, :, part(j)]) + dot(yh[n, part(i), :], xl[n, :, part(j)])) * inverse
            x1 = a_buf[n, part(i), part(j)] * inverse
            x2 = base[n, part(i), part(j)]
            value = C1 * x1 + C2 * x2 + C3 * x3
            if i == j:
                rows = lax.broadcasted_iota(jnp.int32, (HALF, HALF), 0)
                cols = lax.broadcasted_iota(jnp.int32, (HALF, HALF), 1)
                value = value + jnp.where(rows == cols, C0, 0.0)
            base[n, part(i), part(j)] = value
            rest = C4 * x1 + C5 * x2 + C6 * x3
            oh[n, part(i), part(j)] = x3.astype(BF16)
            ol[n, part(i), part(j)] = rest.astype(BF16)
            if i != j:
                oh[n, part(j), part(i)] = x3.T.astype(BF16)
                ol[n, part(j), part(i)] = rest.T.astype(BF16)

    def last(n):
        for i, j in tiles:
            both(xh.at[n], xl.at[n], i, j, base[n, part(i), part(j)] + dot(oh[n, part(i), :], ol[n, :, part(j)]))

    def slot(k):
        live = assign_ref[0, me * 3 + k] >= 0
        graft = jnp.zeros((1, 1), F32)
        for i in range(2):
            for j in range(2):
                piece = held[k, 2 * i:2 * i + 2, :, :, :, :, part(j)].reshape(HALF, HALF) * factor
                graft = graft + total(piece * piece)
                put(sh, sl, i, j, piece)
        nt, tn = ((1,), (1,)), ((0,), (0,))
        squares = (
            stat(0, lbuf, k, live,
                 lambda i, j: dot(sh[part(i), :], sh[part(j), :], nt),
                 lambda i, j: dot(sh[part(i), :], sl[part(j), :], nt)),
            stat(1, rbuf, k, live,
                 lambda i, j: dot(sh[:, part(i)], sh[:, part(j)], tn),
                 lambda i, j: dot(sh[:, part(i)], sl[:, part(j)], tn)))
        norms = [jnp.sqrt(square + 1e-06) for square in squares]
        inverses = [1.0 / norm for norm in norms]
        for n in range(2):
            second(n, inverses[n])
        for n in range(2):
            third(n, inverses[n])
        for n in range(2):
            last(n)
        scale = 1.0 / (jnp.sqrt(jnp.sqrt(norms[0])) * jnp.sqrt(jnp.sqrt(norms[1])))

        th, tl = oh.at[0], ol.at[0]
        for i in range(2):
            for j in range(2):
                put(th, tl, i, j, dot(xh[0, part(i), :], sh[:, part(j)])
                    + (dot(xh[0, part(i), :], sl[:, part(j)]) + dot(xl[0, part(i), :], sh[:, part(j)])))
        square = jnp.zeros((1, 1), F32)
        for i in range(2):
            for j in range(2):
                value = dot(th[part(i), :], xh[1, :, part(j)]) + (
                    dot(th[part(i), :], xl[1, :, part(j)]) + dot(tl[part(i), :], xh[1, :, part(j)]))
                square = square + total(value * value)
                base[0, part(i), part(j)] = value
        count = 512.0 * 512.0
        ratio = scale * jnp.sqrt(graft / count + 1e-12) / jnp.sqrt(square * (scale * scale) / count + 1e-12)
        for i in range(2):
            back[k, 2 * i:2 * i + 2] = (base[0, part(i), :] * ratio).reshape(2, 4, 2, 2, 8, 512)

    def turn(k, carry):
        landed(arrive(k))
        slot(k)
        start(from_slot(k))
        return carry

    lax.fori_loop(0, 3, turn, 0)
    landed(from_slot(0))
    start(in_first())
    landed(from_slot(1))
    landed(from_slot(2))
    lax.fori_loop(0, cap, build_comp, 0, unroll=8)
    start(in_more())
    gone(out_first())
    gone(out_more())
    gone(to_first())
    gone(to_more(1))
    gone(to_more(2))
    for k in range(3):
        gone(from_slot(k))
    for copy in sum_copies + flag_copies:
        copy.wait_send()
    for copies in (in_first(), in_more()):
        landed(copies)
        gone(copies)

    def take(b, carry):
        s = look(OWNER, b, 95)
        _, za, xa, _, _ = place(s)
        for h, a in enumerate((za, xa)):
            entry = look(ENTRY_A + h, s, 7 + cap)
            update_ref[0, b, h * 8:h * 8 + 8] = fin[h, a, entry]
        return carry

    lax.fori_loop(0, update_ref.shape[1], take, 0, unroll=16)


def step(cap, ident, assign, gradient, left_stat, right_stat):
    vm = lambda *shape, dtype=F32: pltpu.VMEM(shape, dtype)
    half = lambda *shape: pltpu.VMEM(shape, BF16)
    dma = lambda *shape: pltpu.SemaphoreType.DMA(shape)
    any_spec = pl.BlockSpec(memory_space=pl.ANY)
    vmem = pl.BlockSpec(memory_space=pltpu.VMEM)
    entries = 8 + cap
    piece = (3, 4, 4, 2, 2, 8, 512)
    return pl.pallas_call(
        functools.partial(step_kernel, cap),
        out_shape=(
            jax.ShapeDtypeStruct(gradient.shape, F32),
            jax.ShapeDtypeStruct(left_stat.shape, F32),
            jax.ShapeDtypeStruct(right_stat.shape, F32),
            jax.ShapeDtypeStruct((1, 1), jnp.int32),
        ),
        in_specs=[any_spec] * 4,
        out_specs=(vmem, vmem, vmem, pl.BlockSpec(memory_space=pltpu.SMEM)),
        scratch_shapes=[
            vm(2, 4, entries, 8, 512), vm(2, 4, entries, 8, 512), vm(2, 2, 8, 4, 8, 512), vm(*piece),
            vm(*piece), vm(3, 2, 8, 4, 8, 512), vm(2, 4, cap, 8, 512), vm(2, 4, entries, 8, 512),
            pltpu.SMEM((1, 96), jnp.int32), vm(1, 96, dtype=jnp.int32), vm(1, 32, 16, 512), vm(4, 8, 128), vm(13, 8, 128), vm(4, 8, 128),
            vm(8, 128), vm(8, 128, dtype=jnp.int32), pltpu.SMEM((8, 128), jnp.int32),
            half(512, 512), half(512, 512), vm(2, 512, 512), vm(2, 512, 512),
            half(2, 512, 512), half(2, 512, 512), half(2, 512, 512), half(2, 512, 512), half(2, 512, 512),
            dma(4, 2, 3), dma(4, 2, 3), dma(6, 2, 7), dma(6, 2, 7), dma(10, 2), dma(13), dma(13), dma(3), dma(3),
            dma(6),
        ],
        name="step" + str(cap),
        compiler_params=pltpu.CompilerParams(collective_id=ident, has_side_effects=True, vmem_limit_bytes=(44 if cap == CAP else 63) * 2**20),
    )(assign, gradient, left_stat, right_stat)


def store_kernel(update_in, left_in, right_in, update_out, left_out, right_out):
    left_out[...] = left_in[...]
    right_out[...] = right_in[...]

    @pl.when(pl.program_id(0) == 0)
    def _():
        update_out[...] = update_in[...]


def store(outs):
    slot_spec = pl.BlockSpec((1, 1, 512, 512), lambda k: (0, k, 0, 0))
    whole = pl.BlockSpec((1, 32, 16, 512), lambda k: (0, 0, 0, 0))
    return pl.pallas_call(
        store_kernel,
        grid=(3,),
        out_shape=tuple(jax.ShapeDtypeStruct(out.shape, out.dtype) for out in outs),
        in_specs=[whole, slot_spec, slot_spec],
        out_specs=(whole, slot_spec, slot_spec),
        name="store",
        compiler_params=pltpu.CompilerParams(vmem_limit_bytes=30 * 2**20),
    )(*outs)


def body(gradient, left_stat, right_stat, assign):
    *outs, over = step(CAP, 0, assign, gradient, left_stat, right_stat)

    def again(_):
        return store(step(FULL, 1, assign, gradient, left_stat, right_stat)[:3])

    return lax.cond(over[0, 0] > 0, again, lambda kept: kept, store(outs))


def solution(mesh):
    placed = P("expert", None, "shard", None)
    slots = P("expert", "shard", None, None)
    return jax.shard_map(
        body,
        mesh=mesh,
        in_specs=(placed, slots, slots, P("expert", None)),
        out_specs=(placed, slots, slots),
        check_vma=False,
    )
```
